512 devices in a mesh: seq: 64 (over z, x, core), head: 8 (over y).
Axes of the slice: x: 4, y: 8, z: 8, core: 2. Of those that a mesh axis runs over, the one named last changes fastest.
Arguments:
- queries: bfloat16 [2, 8192, 1024], P(None, 'seq', 'head'), may hold values from -13 to 13
- key_vectors: bfloat16 [2, 8192, 1024], P(None, 'seq', 'head'), may hold values from -13 to 13
- value_vectors: bfloat16 [2, 8192, 1024], P(None, 'seq', 'head'), may hold values from -6 to 6
- conv_taps: float32 [33, 16], P(None, 'head'), may hold values from -1 to 1
- out_weight: bfloat16 [1024, 2048], P('head'), may hold values from -0.1875 to 0.1875
- out_grad: bfloat16 [2, 8192, 2048], P(None, 'seq', 'head'), may hold values from -16 to 16
Outputs:
- layer_output: bfloat16 [2, 8192, 2048], P(None, 'seq', 'head')
- query_grad: bfloat16 [2, 8192, 1024], P(None, 'seq', 'head')
- key_grad: bfloat16 [2, 8192, 1024], P(None, 'seq', 'head')
- value_grad: bfloat16 [2, 8192, 1024], P(None, 'seq', 'head')
- weight_grad: float32 [1024, 2048], P('head', 'seq')
The draws below stay inside these ranges and needn't reach their ends.
All inputs are finite; a program needn't handle non-finite values.
Results may differ from the reference program's by a relative error of at most 0.0049.
Values may be sent and summed in bfloat16 or wider, within the bound.
No kernel may reach another device: no remote copies, remote signals or barrier semaphores. Data moves between devices by JAX's collectives and lax.ppermute only.
A program may use at most 64 MiB of HBM per device.

```python
import math
from functools import partial
import jax
import jax.numpy as jnp
from jax import lax

D = 2048
HEADS = 16
HD = 64
TAPS = 33
ITERS = 2
LM_DEV = 2
TOK_DEV = 128
NTOK = 8192
LANDMARKS = 128


def shared_field(key):
    comp_key = jax.random.fold_in(key, 0)
    components = jax.random.truncated_normal(comp_key, -3.0, 3.0, (2, LANDMARKS, HEADS * HD), jnp.float32)
    return components


def row_scales(scale_key):
    return jnp.exp(jax.random.uniform(scale_key, (2, NTOK, 1), jnp.float32, math.log(0.3), math.log(3.0)))


def draw_queries(key, part):
    components = shared_field(key)
    key = jax.random.fold_in(key, 11)
    noise_key, scale_key = jax.random.split(key, 2)
    segment = TOK_DEV // LM_DEV
    base = jnp.repeat(components, segment, axis=1)
    noise = jax.random.truncated_normal(noise_key, -3.0, 3.0, (2, NTOK, HEADS * HD), jnp.float32)
    rows = row_scales(scale_key) * (0.8 * base + 0.6 * noise)
    return rows.astype(jnp.bfloat16)


def draw_key_vectors(key, part):
    components = shared_field(key)
    key = jax.random.fold_in(key, 23)
    noise_key, scale_key = jax.random.split(key, 2)
    segment = TOK_DEV // LM_DEV
    base = jnp.repeat(components, segment, axis=1)
    noise = jax.random.truncated_normal(noise_key, -3.0, 3.0, (2, NTOK, HEADS * HD), jnp.float32)
    rows = row_scales(scale_key) * (0.8 * base + 0.6 * noise)
    return rows.astype(jnp.bfloat16)


def with_spikes(values, own_key, source, target, parts, factor):
    owner, partner = [(jnp.arange(values.shape[dim]) // (values.shape[dim] // parts)).reshape([-1 if axis == dim else 1 for axis in range(values.ndim)]) for dim in (source, target)]
    chosen = jax.random.permutation(own_key, parts)[partner]
    strong = (owner == chosen) | (owner == (partner + parts // 2) % parts)
    return jnp.where(strong, factor * values, values)


def block_scale(key, extent, cuts, low, high):
    def one(dim, parts):
        heights = jax.random.uniform(jax.random.fold_in(jax.random.fold_in(key, 6), dim), (parts,), jnp.float32, low / len(cuts), high / len(cuts))
        return jnp.repeat(jnp.exp(heights), extent[dim] // parts).reshape((-1,) + (1,) * (len(extent) - dim - 1))

    loudness = one(*cuts[0])
    for cut in cuts[1:]:
        loudness = loudness * one(*cut)
    return loudness


def normal_values(rng, shape, width, bound, cuts=(), held_as=jnp.bfloat16):
    gain = block_scale(rng, shape, cuts, -0.22, 0.18) if cuts else 1.0
    values = jax.random.normal(rng, shape, jnp.float32) * width * gain
    return jnp.minimum(jnp.maximum(values, -bound), bound).astype(held_as)


def noise_with(rng, dims, spread, most, cuts, heavy, kind=jnp.bfloat16):
    values = spread * jax.random.normal(rng, dims, jnp.float32)
    if cuts:
        values = values * block_scale(rng, dims, cuts, -0.22, 0.18)
    return jnp.clip(with_spikes(values, jax.random.fold_in(rng, 3), *heavy), -most, most).astype(kind)


def setup_inputs(seed: int = 0) -> dict:
    streams_of = jax.random.split(jax.random.key(seed), 7)
    queries = draw_queries(jax.random.fold_in(streams_of[6], 71), 0)
    key_vectors = draw_key_vectors(jax.random.fold_in(streams_of[6], 71), 0)
    value_vectors = normal_values(streams_of[2], (2, NTOK, HEADS * HD), 1.0, 6.0, ((1, 64), (2, 8)))
    conv_taps = normal_values(streams_of[3], (TAPS, HEADS), TAPS ** -0.5, 1.0, ((1, 8),), jnp.float32)
    out_weight = normal_values(streams_of[4], (HEADS * HD, D), (HEADS * HD) ** -0.5, 0.1875, ((0, 8),))
    out_grad = noise_with(streams_of[5], (2, NTOK, D), 1.0, 16.0, ((1, 64), (2, 8)), (1, 2, 64, 4.0))
    return {"queries": queries, "key_vectors": key_vectors, "value_vectors": value_vectors, "conv_taps": conv_taps, "out_weight": out_weight, "out_grad": out_grad}


highest = lax.Precision.HIGHEST

def newton_inverse(matrix):
    column_peak = lax.stop_gradient(lax.optimization_barrier(jnp.max(lax.optimization_barrier(jnp.sum(matrix, axis=-2)), axis=-1)))
    approx = jnp.swapaxes(matrix, -1, -2) / column_peak[..., None, None]
    identity = jnp.eye(matrix.shape[-1], dtype=matrix.dtype)
    for iteration in range(ITERS):
        product = jnp.matmul(matrix, approx, precision=highest)
        factor = 7.0 * identity - product
        factor = 15.0 * identity - jnp.matmul(product, factor, precision=highest)
        factor = 13.0 * identity - jnp.matmul(product, factor, precision=highest)
        approx = 0.25 * jnp.matmul(approx, factor, precision=highest)
    return approx

def convolve(padded, tap_weights, length):
    summed = tap_weights[0] * padded[:, 0:length]
    for offset in range(1, tap_weights.shape[0]):
        summed = summed + tap_weights[offset] * padded[:, offset:offset + length]
    return summed

def attend(query_head, key_head, value_head, tap_weights):
    length = query_head.shape[1]
    score_scale = HD ** (-0.5)
    query_means = query_head.reshape(2, LANDMARKS, length // LANDMARKS, HD).mean(axis=2)
    key_means = key_head.reshape(2, LANDMARKS, length // LANDMARKS, HD).mean(axis=2)
    token_weights = jax.nn.softmax(jnp.einsum('bnd,bmd->bnm', query_head, key_means, precision=highest) * score_scale, axis=-1)
    landmark_weights = jax.nn.softmax(jnp.einsum('bjd,bmd->bjm', query_means, key_means, precision=highest) * score_scale, axis=-1)
    key_weights = jax.nn.softmax(jnp.einsum('bjd,bnd->bjn', query_means, key_head, precision=highest) * score_scale, axis=-1)
    mixed_values = jnp.einsum('bjn,bnd->bjd', key_weights, value_head, precision=highest)
    landmark_mix = jnp.matmul(newton_inverse(landmark_weights), mixed_values, precision=highest)
    rim_width = TAPS // 2
    padded = jnp.pad(value_head, ((0, 0), (rim_width, rim_width), (0, 0)))
    attended = jnp.einsum('bnm,bmd->bnd', token_weights, landmark_mix, precision=highest)
    return attended + convolve(padded, tap_weights, length)

def reference(queries, key_vectors, value_vectors, conv_taps, out_weight, out_grad):
    tokens = queries.shape[1]
    flat_grad = out_grad.reshape(2 * tokens, D)
    context_grad = jnp.dot(flat_grad, out_weight.T, preferred_element_type=jnp.float32)

    def split_heads(array):
        return array.astype(jnp.float32).reshape(2, tokens, HEADS, HD).transpose(2, 0, 1, 3)

    def merge_heads(array):
        return array.transpose(1, 2, 0, 3).reshape(2, tokens, HEADS * HD)

    def per_head(operands):
        query_head, key_head, value_head, tap_head, grad_head = operands
        context, pullback = jax.vjp(partial(attend, tap_weights=tap_head), query_head, key_head, value_head)
        grads = pullback(grad_head)
        return (context, grads[0], grads[1], grads[2])
    contexts, query_part, key_part, value_part = lax.map(per_head, (split_heads(queries), split_heads(key_vectors), split_heads(value_vectors), conv_taps.T, split_heads(context_grad.reshape(2, tokens, HEADS * HD))))
    context_b = merge_heads(contexts).astype(jnp.bfloat16).reshape(2 * tokens, HEADS * HD)
    layer_output = jnp.dot(context_b, out_weight, preferred_element_type=jnp.float32).astype(jnp.bfloat16).reshape(2, tokens, D)
    weight_grad = jnp.dot(context_b.T, flat_grad, preferred_element_type=jnp.float32)
    return (layer_output, merge_heads(query_part).astype(jnp.bfloat16), merge_heads(key_part).astype(jnp.bfloat16), merge_heads(value_part).astype(jnp.bfloat16), weight_grad)
```

```python
import functools

import jax
import jax.numpy as jnp
from jax import lax
from jax.experimental import pallas as pl
from jax.experimental.pallas import tpu as pltpu
from jax.sharding import PartitionSpec as P

ITERS = 2
SEGS = 2
f32 = jnp.float32
bf16 = jnp.bfloat16
PIECES = ((0,), (2, 6), (1, 3), (7, 5), (4,))
NN = (((1,), (0,)), ((), ()))
NT = (((1,), (1,)), ((), ()))


def dot(left, right, dims=NN):
    return lax.dot_general(left, right, dims, preferred_element_type=f32)


def halves(value):
    if value.dtype == bf16:
        return (value,)
    high = value.astype(bf16)
    return high, (value - high.astype(f32)).astype(bf16)


def prod(left, right, dims=NN):
    left = left if isinstance(left, tuple) else halves(left)
    right = right if isinstance(right, tuple) else halves(right)
    total = dot(left[0], right[0], dims)
    if len(right) > 1:
        total = total + dot(left[0], right[1], dims)
    if len(left) > 1:
        total = total + dot(left[1], right[0], dims)
    return total


def block_at(shift, parts):
    core = lax.rem(lax.axis_index("seq"), 2)
    step = jnp.where(core == 0, parts - shift, parts + shift)
    return lax.rem(lax.axis_index("head") + step, parts)


def first_head(shape):
    return lax.broadcasted_iota(jnp.int32, shape, 1) < shape[1] // 2


def stack(rows):
    mask = first_head(rows.shape)
    zero = jnp.zeros_like(rows)
    return jnp.concatenate([jnp.where(mask, rows, zero), jnp.where(mask, zero, rows)], axis=0)


def own_blocks(full):
    count = full.shape[0] // 2
    mask = first_head((count, full.shape[1]))
    zero = jnp.zeros((count, full.shape[1]), full.dtype)
    return jnp.concatenate(
        [jnp.where(mask, full[:count], zero), jnp.where(mask, zero, full[count:])], axis=0
    )


def pick(full):
    count = full.shape[0] // 2
    return jnp.where(first_head((count, full.shape[1])), full[:count], full[count:])


def marks(ref, row, groups, stride):
    return jnp.concatenate(
        [ref[pl.ds(row + seg, groups, stride=stride), :] for seg in range(SEGS)], axis=0
    )


def means_kernel(q_ref, k_ref, out_ref):
    documents, tokens, _ = q_ref.shape
    segment = tokens // SEGS
    rows = []
    for ref in (q_ref, k_ref):
        for doc in range(documents):
            for seg in range(SEGS):
                part = ref[doc, seg * segment : (seg + 1) * segment, :].astype(f32)
                rows.append(jnp.sum(part, axis=0, keepdims=True) * (1.0 / segment))
    block = jnp.concatenate(rows, axis=0)
    out_ref[...] = jnp.broadcast_to(block[None], out_ref.shape)


def stats_kernel(scale, got_ref, q_ref, k_ref, v_ref, t_ref, s_ref, o_ref, log_ref, qm_ref, km_ref):
    documents = q_ref.shape[0]
    groups = got_ref.shape[0] // 8
    count = SEGS * groups
    logs = []
    for doc in range(documents):
        qm = marks(got_ref, doc * SEGS, groups, 8)
        km = marks(got_ref, 4 + doc * SEGS, groups, 8)
        qm_ref[doc] = qm
        km_ref[doc] = km
        scores = prod(q_ref[doc], stack(km), NT) * scale
        for head in range(2):
            part = scores[:, head * count : (head + 1) * count]
            part = jnp.exp(part - jnp.max(part, axis=1, keepdims=True))
            t_ref[doc, :, head * count : (head + 1) * count] = part / jnp.sum(
                part, axis=1, keepdims=True
            )
        scores = prod(k_ref[doc], stack(qm), NT) * scale
        s_ref[doc] = scores
        peak = jnp.max(scores, axis=0, keepdims=True)
        part = jnp.exp(scores - peak)
        total = jnp.sum(part, axis=0, keepdims=True)
        o_ref[doc] = pick(prod((part / total).T, v_ref[doc]))
        log = peak + jnp.log(total)
        logs += [log[:, :count], log[:, count:]]
    logs.append(jnp.zeros((8 - len(logs), count), f32))
    log_ref[...] = jnp.concatenate(logs, axis=0)


def chunk_kernel(parts, rim, *refs):
    og_refs = refs[:parts]
    w_ref, v_ref, t_ref, o_ref, log_ref = refs[parts : parts + 5]
    out_ref, cg_ref, head_ref, tail_ref = refs[parts + 5 : parts + 9]
    documents, tokens, channels = cg_ref.shape
    groups = out_ref.shape[0] // 16
    width = w_ref.shape[1] // parts

    def columns(shift):
        return pl.ds(pl.multiple_of(block_at(shift, parts) * width, width), width)

    total = None
    for shift in range(parts):
        part = dot(og_refs[shift][...], w_ref[:, columns(shift)], NT)
        total = part if total is None else total + part
    for ref, shifts in zip(refs[parts + 9 :], PIECES):
        for slot, shift in enumerate(shifts):
            ref[slot] = w_ref[:, columns(-shift)]
    for doc in range(documents):
        grad = total[doc * tokens : (doc + 1) * tokens]
        cg_ref[doc] = grad
        for ref, rows in ((head_ref, slice(0, rim)), (tail_ref, slice(tokens - rim, tokens))):
            high, low = halves(grad[rows])
            ref[doc, 0:rim, :] = v_ref[doc, rows, :]
            ref[doc, rim : 2 * rim, :] = high
            ref[doc, 2 * rim : 3 * rim, :] = low
        mix = pick(prod(t_ref[doc].T, grad))
        for seg in range(SEGS):
            row = doc * SEGS + seg
            rows = slice(seg * groups, (seg + 1) * groups)
            out_ref[pl.ds(row, groups, stride=16), :] = o_ref[doc, rows, :]
            out_ref[pl.ds(4 + row, groups, stride=16), :] = mix[rows]
    for row in range(8):
        out_ref[pl.ds(8 + row, groups, stride=16), :] = jnp.broadcast_to(
            log_ref[row : row + 1, :], (groups, channels)
        )


def newton_kernel(scale, parts, *refs):
    og_refs = refs[:parts]
    qm_ref, km_ref, ogt_ref, a_ref, z_ref, p_ref, f2_ref, f3_ref, inv_ref = refs[parts:]
    documents, count, _ = qm_ref.shape
    width = og_refs[0].shape[1]
    for shift in range(parts):
        block = block_at(shift, parts)
        ogt_ref[pl.ds(pl.multiple_of(block * width, width), width), :] = og_refs[shift][...].T
    row = lax.broadcasted_iota(jnp.int32, (count, count), 0)
    identity = (row == lax.broadcasted_iota(jnp.int32, (count, count), 1)).astype(f32)
    units = []
    for doc in range(documents):
        scores = prod(stack(qm_ref[doc]), km_ref[doc], NT) * scale
        scores = jnp.exp(scores - jnp.max(scores, axis=1, keepdims=True))
        scores = scores / jnp.sum(scores, axis=1, keepdims=True)
        units += [scores[:count], scores[count:]]
    approx = []
    for index, unit in enumerate(units):
        a_ref[index] = unit
        sums = jnp.sum(unit, axis=0, keepdims=True)
        approx.append(unit.T / jnp.max(sums, axis=1, keepdims=True))
    units = [halves(unit) for unit in units]
    every = range(len(units))
    for step in range(ITERS):
        for i in every:
            z_ref[step, i] = approx[i]
        spread = [halves(approx[i]) for i in every]
        product = [prod(units[i], spread[i]) for i in every]
        for i in every:
            p_ref[step, i] = product[i]
        factor = [7.0 * identity - product[i] for i in every]
        product = [halves(product[i]) for i in every]
        factor = [15.0 * identity - prod(product[i], factor[i]) for i in every]
        for i in every:
            f2_ref[step, i] = factor[i]
        factor = [13.0 * identity - prod(product[i], factor[i]) for i in every]
        for i in every:
            f3_ref[step, i] = factor[i]
        approx = [0.25 * prod(spread[i], factor[i]) for i in every]
    for i in every:
        inv_ref[i] = approx[i]


def combine_kernel(got_ref, out_ref, log_ref):
    groups = got_ref.shape[0] // 16
    channels = got_ref.shape[1]
    me = lax.axis_index("seq")
    lane = lax.broadcasted_iota(jnp.int32, (groups, channels), 1)
    shares, logs = [], []
    for unit in range(4):
        log = got_ref[pl.ds(8 + unit, groups, stride=16), :]
        top = jnp.max(log, axis=0, keepdims=True)
        part = jnp.exp(log - top)
        total = jnp.sum(part, axis=0, keepdims=True)
        logs.append(top + jnp.log(total))
        shares.append(part / total)
    logs.append(jnp.zeros((4, channels), f32))
    log_ref[...] = jnp.concatenate(logs, axis=0)
    mixed, mix = [], []
    for doc in range(2):
        for seg in range(SEGS):
            row = doc * SEGS + seg
            weight = [
                jnp.sum(
                    jnp.where(lane == seg * groups + me, shares[doc * 2 + head], 0.0),
                    axis=1,
                    keepdims=True,
                )
                for head in range(2)
            ]
            weight = jnp.where(lane < channels // 2, weight[0], weight[1])
            mixed.append(
                jnp.sum(weight * got_ref[pl.ds(row, groups, stride=16), :], axis=0, keepdims=True)
            )
            mix.append(jnp.sum(got_ref[pl.ds(4 + row, groups, stride=16), :], axis=0, keepdims=True))
    block = jnp.concatenate(mixed + mix, axis=0)
    out_ref[...] = jnp.broadcast_to(block[None], out_ref.shape)


def conv_kernel(taps_ref, v_ref, cg_ref, above_ref, below_ref, conv_ref, back_ref, vp, cp):
    documents, tokens, channels = v_ref.shape
    taps = taps_ref.shape[0]
    rim = taps // 2
    for doc in range(documents):
        vp[doc, rim : rim + tokens, :] = v_ref[doc].astype(f32)
        cp[doc, rim : rim + tokens, :] = cg_ref[doc]
        for ref, start in ((above_ref, 0), (below_ref, rim + tokens)):
            rows = [ref[doc, i * rim : (i + 1) * rim, :].astype(f32) for i in range(3)]
            vp[doc, start : start + rim, :] = rows[0]
            cp[doc, start : start + rim, :] = rows[1] + rows[2]
    lane = lax.broadcasted_iota(jnp.int32, (1, channels), 1)
    for doc in range(documents):
        conv = jnp.zeros((tokens, channels), f32)
        back = jnp.zeros((tokens, channels), f32)
        for tap in range(taps):
            weight = jnp.where(lane < channels // 2, taps_ref[tap, 0], taps_ref[tap, 1])
            conv = conv + weight * vp[doc, tap : tap + tokens, :]
            start = 2 * rim - tap
            back = back + weight * cp[doc, start : start + tokens, :]
        conv_ref[doc] = conv
        back_ref[doc] = back


def context_kernel(got_ref, t_ref, inv_ref, conv_ref, ctx_ref, mixed_ref, mix_ref, lm_ref):
    documents, tokens, _ = conv_ref.shape
    groups = got_ref.shape[0] // 8
    for doc in range(documents):
        mixed = marks(got_ref, doc * SEGS, groups, 8)
        mixed_ref[doc] = mixed
        mix_ref[doc] = marks(got_ref, 4 + doc * SEGS, groups, 8)
        inverse = jnp.concatenate([inv_ref[doc * 2], inv_ref[doc * 2 + 1]], axis=0)
        landmark = own_blocks(prod(inverse, mixed))
        lm_ref[doc] = landmark
        ctx = (prod(t_ref[doc], landmark) + conv_ref[doc]).astype(bf16)
        ctx_ref[doc * tokens : (doc + 1) * tokens, :] = ctx


def main_kernel(
    scale, log_ref, t_ref, s_ref, cg_ref, qm_ref, km_ref, inv_ref, q_ref, k_ref, v_ref,
    back_ref, ogt_ref, ctx_ref, mixed_ref, mix_ref, lm_ref, out_ref, qd_ref, kd_ref, vg_ref, held,
):
    documents, tokens, channels = q_ref.shape
    count = qm_ref.shape[1]
    groups = count // SEGS
    for doc in range(documents):
        mixed = mixed_ref[doc]
        weights = t_ref[doc]
        upstream = prod(cg_ref[doc], lm_ref[doc], NT)
        back = weights * upstream
        back = jnp.concatenate(
            [
                back[:, part] - weights[:, part] * jnp.sum(back[:, part], axis=1, keepdims=True)
                for part in (slice(0, count), slice(count, 2 * count))
            ],
            axis=1,
        ) * scale
        qd_ref[doc] = prod(back, stack(km_ref[doc]))
        key_terms = pick(prod(back.T, q_ref[doc]))
        turned = jnp.concatenate([inv_ref[doc * 2].T, inv_ref[doc * 2 + 1].T], axis=0)
        mixed_grad = own_blocks(prod(turned, mix_ref[doc]))
        ones = jnp.ones((8, channels), bf16)
        mixed_dot = prod(ones, mixed_grad * stack(mixed), NT)[0:1]
        mixed_grad = halves(mixed_grad)
        log = jnp.concatenate(
            [log_ref[doc * 2 : doc * 2 + 1, :], log_ref[doc * 2 + 1 : doc * 2 + 2, :]], axis=1
        )
        key_weights = jnp.exp(s_ref[doc] - log)
        key_back = key_weights * (prod(v_ref[doc], mixed_grad, NT) - mixed_dot) * scale
        query_terms = pick(prod(key_back.T, k_ref[doc]))
        kd_ref[doc] = prod(key_back, stack(qm_ref[doc]))
        vg_ref[doc] = (prod(key_weights, mixed_grad) + back_ref[doc]).astype(bf16)
        for base, terms in ((0, query_terms), (4, key_terms)):
            high = terms.astype(bf16).astype(f32)
            low = terms - high
            for seg in range(SEGS):
                row = base + doc * SEGS + seg
                rows = slice(seg * groups, (seg + 1) * groups)
                held[pl.ds(row, groups, stride=16), :] = high[rows]
                held[pl.ds(8 + row, groups, stride=16), :] = low[rows]
    out_ref[:, 0:16, :] = held[...].astype(bf16).reshape(groups, 16, channels)
    terms = dot(ogt_ref[...], ctx_ref[...]).astype(bf16)
    out_ref[:, 16:, :] = terms.reshape(groups, terms.shape[0] // groups, channels)


def newton_back_kernel(
    scale, a_ref, z_ref, p_ref, f2_ref, f3_ref, qm_ref, km_ref, mixed_ref, mix_ref, out_ref, held
):
    documents, count, channels = qm_ref.shape
    me = lax.axis_index("seq")
    groups = count // SEGS
    row = lax.broadcasted_iota(jnp.int32, (count, count), 0)
    identity = (row == lax.broadcasted_iota(jnp.int32, (count, count), 1)).astype(f32)
    every = range(documents * 2)
    down = []
    for doc in range(documents):
        full = prod(stack(mix_ref[doc]), mixed_ref[doc], NT)
        down += [full[:count], full[count:]]
    unit_t = [halves(a_ref[i].T) for i in every]
    grads = [None for i in every]
    for step in reversed(range(ITERS)):
        down = [halves(0.25 * down[i]) for i in every]
        turned = [halves(z_ref[step, i].T) for i in every]
        product = [p_ref[step, i] for i in every]
        product_t = [halves(product[i].T) for i in every]
        third = [prod(turned[i], down[i]) for i in every]
        third = [halves(third[i]) for i in every]
        carry = [prod(down[i], f3_ref[step, i].T) for i in every]
        second = [-prod(product_t[i], third[i]) for i in every]
        second = [halves(second[i]) for i in every]
        first = [-prod(product_t[i], second[i]) for i in every]
        flow = [
            -first[i]
            - prod(third[i], f2_ref[step, i].T)
            - prod(second[i], (7.0 * identity - product[i]).T)
            for i in every
        ]
        flow = [halves(flow[i]) for i in every]
        more = [prod(flow[i], turned[i]) for i in every]
        grads = [more[i] if grads[i] is None else grads[i] + more[i] for i in every]
        down = [carry[i] + prod(unit_t[i], flow[i]) for i in every]
    for doc in range(documents):
        back, turned = [], []
        for head in range(2):
            i = doc * 2 + head
            unit = a_ref[i]
            peak = jnp.max(jnp.sum(unit, axis=0, keepdims=True), axis=1, keepdims=True)
            grad = grads[i] + down[i].T / peak
            part = unit * grad
            part = (part - unit * jnp.sum(part, axis=1, keepdims=True)) * scale
            back.append(part)
            turned.append(part.T)
        held[doc] = pick(prod(jnp.concatenate(back, axis=0), km_ref[doc]))
        held[documents + doc] = pick(prod(jnp.concatenate(turned, axis=0), qm_ref[doc]))
    for kind in range(2 * documents):
        for seg in range(SEGS):
            out_row = kind * SEGS + seg
            out_ref[out_row : out_row + 1, :] = held[kind, pl.ds(seg * groups + me, 1), :]


def finish_kernel(got_ref, own_ref, qd_ref, kd_ref, qg_ref, kg_ref, wg_ref):
    documents, tokens, _ = qd_ref.shape
    segment = tokens // SEGS
    total = jnp.sum(got_ref[:, 0:16, :].astype(f32), axis=0)
    total = (total[0:8] + total[8:16] + own_ref[...]) * (1.0 / segment)
    for base, source, target in ((0, qd_ref, qg_ref), (4, kd_ref, kg_ref)):
        for doc in range(documents):
            for seg in range(SEGS):
                row = base + doc * SEGS + seg
                rows = slice(seg * segment, (seg + 1) * segment)
                target[doc, rows, :] = (source[doc, rows, :] + total[row : row + 1]).astype(bf16)
    wg_ref[...] = jnp.sum(got_ref[:, 16:, :].astype(f32), axis=0)


def output_kernel(blocks, weights, *refs):
    total = None
    tokens = refs[-1].shape[0]
    for (index, block), (source, slot) in zip(blocks, weights):
        part = dot(refs[index][block * tokens : (block + 1) * tokens, :], refs[source][slot])
        total = part if total is None else total + part
    refs[-1][...] = total.astype(bf16)


def call(kernel, outs, *operands, scratch=(), smem=(), flops=1e8, size=2e6):
    vmem = pl.BlockSpec(memory_space=pltpu.VMEM)
    scalar = pl.BlockSpec(memory_space=pltpu.SMEM)
    return pl.pallas_call(
        kernel,
        out_shape=[jax.ShapeDtypeStruct(shape, kind) for shape, kind in outs],
        in_specs=[scalar if i in smem else vmem for i in range(len(operands))],
        out_specs=[vmem for _ in outs],
        scratch_shapes=list(scratch),
        compiler_params=pltpu.CompilerParams(vmem_limit_bytes=16 * 1024 * 1024),
        cost_estimate=pl.CostEstimate(
            flops=int(flops), bytes_accessed=int(size), transcendentals=0
        ),
    )(*operands)


def exchange(blocks, axis):
    return lax.all_to_all(blocks, axis, 0, 0, tiled=True)


def shift_by(block, shift, parts):
    pairs = []
    for i in range(lax.axis_size("seq")):
        step = shift if i % 2 == 0 else parts - shift
        pairs += [(i * parts + j, i * parts + (j + step) % parts) for j in range(parts)]
    return lax.ppermute(block, ("seq", "head"), pairs)


def gathered(block, parts):
    return [block] + [shift_by(block, shift, parts) for shift in range(1, parts)]


def shards(queries, key_vectors, value_vectors, conv_taps, out_weight, out_grad):
    documents, tokens, channels = queries.shape
    heads = conv_taps.shape[1]
    groups = lax.axis_size("seq")
    parts = lax.axis_size("head")
    count = SEGS * groups
    scale = (channels // heads) ** (-0.5)
    rim = conv_taps.shape[0] // 2
    model_width = out_weight.shape[1]
    own_width = model_width // parts
    column_rows = model_width // groups
    rows_shape = (documents, tokens, channels)
    marks_shape = (documents, count, channels)
    pair_shape = (documents, tokens, 2 * count)
    units = 2 * documents
    saved = (ITERS, units, count, count)

    (sent,) = call(means_kernel, [((groups, 8, channels), f32)], queries, key_vectors)
    own_grad, sent = lax.optimization_barrier((out_grad, sent))
    got = exchange(sent, "seq").reshape(groups * 8, channels)
    og_parts = gathered(own_grad.reshape(documents * tokens, own_width), parts)

    weights, scores, local_mixed, local_log, qm, km = call(
        functools.partial(stats_kernel, scale),
        [
            (pair_shape, f32),
            (pair_shape, f32),
            (marks_shape, f32),
            ((8, count), f32),
            (marks_shape, f32),
            (marks_shape, f32),
        ],
        got, queries, key_vectors, value_vectors,
    )
    sent, context_grad, first_rows, last_rows, *pieces = call(
        functools.partial(chunk_kernel, parts, rim),
        [((groups * 16, channels), f32), (rows_shape, f32)]
        + [((documents, 3 * rim, channels), bf16)] * 2
        + [((len(shifts), channels, own_width), bf16) for shifts in PIECES],
        *og_parts, out_weight, value_vectors, weights, local_mixed, local_log,
    )
    got = exchange(sent, "seq")
    ends = groups - 1
    above = lax.ppermute(last_rows, "seq", [(i, i + 1) for i in range(ends)])
    below = lax.ppermute(first_rows, "seq", [(i + 1, i) for i in range(ends)])
    kept, stay, up, down, across = pieces
    up = shift_by(up, 1, parts)
    down = shift_by(down, parts - 1, parts)
    across = shift_by(across, 4, parts)
    og_turned, a, z, p, f2, f3, inverse = call(
        functools.partial(newton_kernel, scale, parts),
        [((model_width, documents * tokens), bf16), ((units, count, count), f32)]
        + [(saved, f32)] * 4
        + [((units, count, count), f32)],
        *og_parts, qm, km,
        flops=3e9,
    )
    got, up, down, across, above, below, inverse = lax.optimization_barrier(
        (got, up, down, across, above, below, inverse)
    )
    sent, logs = call(
        combine_kernel, [((groups, 8, channels), f32), ((8, count), f32)], got
    )
    sent, up, down, stay = lax.optimization_barrier((sent, up, down, stay))
    got = exchange(sent, "seq").reshape(groups * 8, channels)
    conv, back = call(
        conv_kernel,
        [(rows_shape, f32), (rows_shape, f32)],
        conv_taps, value_vectors, context_grad, above, below,
        scratch=[pltpu.VMEM((documents, tokens + 2 * rim, channels), f32)] * 2,
        smem=(0,),
        flops=1e9,
    )
    up_two = shift_by(jnp.concatenate([stay[0:1], up[1:2]], axis=0), 2, parts)
    down_two = shift_by(jnp.concatenate([stay[1:2], down[1:2]], axis=0), parts - 2, parts)
    got, up_two, down_two, conv, back = lax.optimization_barrier(
        (got, up_two, down_two, conv, back)
    )
    weight_parts = [kept, up, down, across, up_two, down_two]
    context_b, mixed, mix, landmark_mix = call(
        context_kernel,
        [
            ((documents * tokens, channels), bf16),
            (marks_shape, f32),
            (marks_shape, f32),
            ((documents, 2 * count, channels), f32),
        ],
        got, weights, inverse, conv,
    )
    near = [shift_by(context_b, 1, parts), shift_by(context_b, parts - 1, parts)]
    sent, query_direct, key_direct, value_grad = call(
        functools.partial(main_kernel, scale),
        [
            ((groups, 16 + column_rows, channels), bf16),
            (rows_shape, f32),
            (rows_shape, f32),
            (rows_shape, bf16),
        ],
        logs, weights, scores, context_grad, qm, km, inverse, queries, key_vectors,
        value_vectors, back, og_turned, context_b, mixed, mix, landmark_mix,
        scratch=[pltpu.VMEM((groups * 16, channels), f32)],
        flops=1e9,
    )
    sent, near, mix = lax.optimization_barrier((sent, near, mix))
    got = exchange(sent, "seq")
    far = [
        shift_by(jnp.concatenate([near[0], context_b, near[1]], axis=0), 3, parts),
        shift_by(jnp.concatenate([near[0], context_b], axis=0), parts - 3, parts),
    ]
    (own,) = call(
        functools.partial(newton_back_kernel, scale),
        [((8, channels), f32)],
        a, z, p, f2, f3, qm, km, mixed, mix,
        scratch=[pltpu.VMEM((2 * documents, count, channels), f32)],
        flops=5e9,
    )
    blocks = ((0, 0), (1, 0), (3, 2), (3, 1), (3, 0), (4, 1), (4, 0), (2, 0))
    slots = ((5, 0), (6, 0), (9, 0), (9, 1), (8, 0), (10, 1), (10, 0), (7, 0))
    (layer_output,) = call(
        functools.partial(output_kernel, blocks, slots),
        [((documents * tokens, own_width), bf16)],
        context_b, *near, *far, *weight_parts,
    )
    query_grad, key_grad, weight_grad = call(
        finish_kernel,
        [(rows_shape, bf16), (rows_shape, bf16), ((column_rows, channels), f32)],
        got, own, query_direct, key_direct,
    )
    return (
        layer_output.reshape(documents, tokens, own_width),
        query_grad,
        key_grad,
        value_grad,
        weight_grad.T,
    )


def solution(mesh):
    in_specs = (
        P(None, "seq", "head"),
        P(None, "seq", "head"),
        P(None, "seq", "head"),
        P(None, "head"),
        P("head", None),
        P(None, "seq", "head"),
    )
    out_specs = (
        P(None, "seq", "head"),
        P(None, "seq", "head"),
        P(None, "seq", "head"),
        P(None, "seq", "head"),
        P("head", "seq"),
    )
    return jax.shard_map(shards, mesh=mesh, in_specs=in_specs, out_specs=out_specs, check_vma=False)
```

```python
import functools

import jax
import jax.numpy as jnp
from jax import lax
from jax.experimental import pallas as pl
from jax.experimental.pallas import tpu as pltpu
from jax.sharding import PartitionSpec as P

ITERS = 2
SEGS = 2
f32 = jnp.float32
bf16 = jnp.bfloat16
PIECES = ((0,), (2, 6), (1, 3), (7, 5), (4,))
NN = (((1,), (0,)), ((), ()))
NT = (((1,), (1,)), ((), ()))


def dot(left, right, dims=NN):
    return lax.dot_general(left, right, dims, preferred_element_type=f32)


def halves(value):
    if value.dtype == bf16:
        return (value,)
    high = value.astype(bf16)
    return high, (value - high.astype(f32)).astype(bf16)


def prod(left, right, dims=NN):
    left = left if isinstance(left, tuple) else halves(left)
    right = right if isinstance(right, tuple) else halves(right)
    total = dot(left[0], right[0], dims)
    if len(right) > 1:
        total = total + dot(left[0], right[1], dims)
    if len(left) > 1:
        total = total + dot(left[1], right[0], dims)
    return total


def block_at(shift, parts):
    core = lax.rem(lax.axis_index("seq"), 2)
    step = jnp.where(core == 0, parts - shift, parts + shift)
    return lax.rem(lax.axis_index("head") + step, parts)


def first_head(shape):
    return lax.broadcasted_iota(jnp.int32, shape, 1) < shape[1] // 2


def stack(rows):
    mask = first_head(rows.shape)
    zero = jnp.zeros_like(rows)
    return jnp.concatenate([jnp.where(mask, rows, zero), jnp.where(mask, zero, rows)], axis=0)


def own_blocks(full):
    count = full.shape[0] // 2
    mask = first_head((count, full.shape[1]))
    zero = jnp.zeros((count, full.shape[1]), full.dtype)
    return jnp.concatenate(
        [jnp.where(mask, full[:count], zero), jnp.where(mask, zero, full[count:])], axis=0
    )


def pick(full):
    count = full.shape[0] // 2
    return jnp.where(first_head((count, full.shape[1])), full[:count], full[count:])


def marks(ref, row, groups, stride):
    return jnp.concatenate(
        [ref[pl.ds(row + seg, groups, stride=stride), :] for seg in range(SEGS)], axis=0
    )


def means_kernel(q_ref, k_ref, out_ref):
    documents, tokens, _ = q_ref.shape
    segment = tokens // SEGS
    rows = []
    for ref in (q_ref, k_ref):
        for doc in range(documents):
            for seg in range(SEGS):
                part = ref[doc, seg * segment : (seg + 1) * segment, :].astype(f32)
                rows.append(jnp.sum(part, axis=0, keepdims=True) * (1.0 / segment))
    block = jnp.concatenate(rows, axis=0)
    out_ref[...] = jnp.broadcast_to(block[None], out_ref.shape)


def stats_kernel(scale, got_ref, q_ref, k_ref, v_ref, t_ref, s_ref, o_ref, log_ref, qm_ref, km_ref):
    documents = q_ref.shape[0]
    groups = got_ref.shape[0] // 8
    count = SEGS * groups
    logs = []
    for doc in range(documents):
        qm = marks(got_ref, doc * SEGS, groups, 8)
        km = marks(got_ref, 4 + doc * SEGS, groups, 8)
        qm_ref[doc] = qm
        km_ref[doc] = km
        scores = prod(q_ref[doc], stack(km), NT) * scale
        for head in range(2):
            part = scores[:, head * count : (head + 1) * count]
            part = jnp.exp(part - jnp.max(part, axis=1, keepdims=True))
            t_ref[doc, :, head * count : (head + 1) * count] = part / jnp.sum(
                part, axis=1, keepdims=True
            )
        scores = prod(k_ref[doc], stack(qm), NT) * scale
        s_ref[doc] = scores
        peak = jnp.max(scores, axis=0, keepdims=True)
        part = jnp.exp(scores - peak)
        total = jnp.sum(part, axis=0, keepdims=True)
        o_ref[doc] = pick(prod((part / total).T, v_ref[doc]))
        log = peak + jnp.log(total)
        logs += [log[:, :count], log[:, count:]]
    logs.append(jnp.zeros((8 - len(logs), count), f32))
    log_ref[...] = jnp.concatenate(logs, axis=0)


def chunk_kernel(parts, rim, *refs):
    og_refs = refs[:parts]
    w_ref, v_ref, t_ref, o_ref, log_ref = refs[parts : parts + 5]
    out_ref, cg_ref, head_ref, tail_ref = refs[parts + 5 : parts + 9]
    documents, tokens, channels = cg_ref.shape
    groups = out_ref.shape[0] // 16
    width = w_ref.shape[1] // parts

    def columns(shift):
        return pl.ds(pl.multiple_of(block_at(shift, parts) * width, width), width)

    total = None
    for shift in range(parts):
        part = dot(og_refs[shift][...], w_ref[:, columns(shift)], NT)
        total = part if total is None else total + part
    for ref, shifts in zip(refs[parts + 9 :], PIECES):
        for slot, shift in enumerate(shifts):
            ref[slot] = w_ref[:, columns(-shift)]
    for doc in range(documents):
        grad = total[doc * tokens : (doc + 1) * tokens]
        cg_ref[doc] = grad
        for ref, rows in ((head_ref, slice(0, rim)), (tail_ref, slice(tokens - rim, tokens))):
            high, low = halves(grad[rows])
            ref[doc, 0:rim, :] = v_ref[doc, rows, :]
            ref[doc, rim : 2 * rim, :] = high
            ref[doc, 2 * rim : 3 * rim, :] = low
        mix = pick(prod(t_ref[doc].T, grad))
        for seg in range(SEGS):
            row = doc * SEGS + seg
            rows = slice(seg * groups, (seg + 1) * groups)
            out_ref[pl.ds(row, groups, stride=16), :] = o_ref[doc, rows, :]
            out_ref[pl.ds(4 + row, groups, stride=16), :] = mix[rows]
    for row in range(8):
        out_ref[pl.ds(8 + row, groups, stride=16), :] = jnp.broadcast_to(
            log_ref[row : row + 1, :], (groups, channels)
        )


def landmark_units(scale, qm_ref, km_ref):
    count = qm_ref.shape[1]
    units = []
    for doc in range(qm_ref.shape[0]):
        scores = prod(stack(qm_ref[doc]), km_ref[doc], NT) * scale
        scores = jnp.exp(scores - jnp.max(scores, axis=1, keepdims=True))
        scores = scores / jnp.sum(scores, axis=1, keepdims=True)
        units += [scores[:count], scores[count:]]
    return units


def column_peak(unit):
    return jnp.max(jnp.sum(unit, axis=0, keepdims=True), axis=1, keepdims=True)


def newton(units, keep):
    every = range(len(units))
    count = units[0].shape[0]
    row = lax.broadcasted_iota(jnp.int32, (count, count), 0)
    identity = (row == lax.broadcasted_iota(jnp.int32, (count, count), 1)).astype(f32)
    approx = [unit.T / column_peak(unit) for unit in units]
    units = [halves(unit) for unit in units]
    for step in range(ITERS):
        spread = [halves(approx[i]) for i in every]
        product = [prod(units[i], spread[i]) for i in every]
        first = [7.0 * identity - product[i] for i in every]
        split = [halves(product[i]) for i in every]
        second = [15.0 * identity - prod(split[i], first[i]) for i in every]
        third = [13.0 * identity - prod(split[i], second[i]) for i in every]
        for i in every:
            keep(step, i, (approx[i], product[i], first[i], second[i], third[i]))
        if step < ITERS - 1 or not keep.last:
            approx = [0.25 * prod(spread[i], third[i]) for i in every]
    return approx


class Nothing:
    last = False

    def __call__(self, step, index, values):
        pass


class Kept:
    last = True

    def __init__(self, refs):
        self.refs = refs

    def __call__(self, step, index, values):
        for ref, value in zip(self.refs, values):
            ref[step, index] = value.T


def inverse_kernel(scale, qm_ref, km_ref, inv_ref):
    for index, unit in enumerate(newton(landmark_units(scale, qm_ref, km_ref), Nothing())):
        inv_ref[index] = unit


def turn_kernel(parts, *refs):
    width = refs[0].shape[1]
    for shift in range(parts):
        start = pl.multiple_of(block_at(shift, parts) * width, width)
        refs[parts][pl.ds(start, width), :] = refs[shift][...].T


def combine_kernel(got_ref, out_ref, log_ref):
    groups = got_ref.shape[0] // 16
    channels = got_ref.shape[1]
    me = lax.axis_index("seq")
    lane = lax.broadcasted_iota(jnp.int32, (groups, channels), 1)
    shares, logs = [], []
    for unit in range(4):
        log = got_ref[pl.ds(8 + unit, groups, stride=16), :]
        top = jnp.max(log, axis=0, keepdims=True)
        part = jnp.exp(log - top)
        total = jnp.sum(part, axis=0, keepdims=True)
        logs.append(top + jnp.log(total))
        shares.append(part / total)
    logs.append(jnp.zeros((4, channels), f32))
    log_ref[...] = jnp.concatenate(logs, axis=0)
    mixed, mix = [], []
    for doc in range(2):
        for seg in range(SEGS):
            row = doc * SEGS + seg
            weight = [
                jnp.sum(
                    jnp.where(lane == seg * groups + me, shares[doc * 2 + head], 0.0),
                    axis=1,
                    keepdims=True,
                )
                for head in range(2)
            ]
            weight = jnp.where(lane < channels // 2, weight[0], weight[1])
            mixed.append(
                jnp.sum(weight * got_ref[pl.ds(row, groups, stride=16), :], axis=0, keepdims=True)
            )
            mix.append(jnp.sum(got_ref[pl.ds(4 + row, groups, stride=16), :], axis=0, keepdims=True))
    block = jnp.concatenate(mixed + mix, axis=0)
    out_ref[...] = jnp.broadcast_to(block[None], out_ref.shape)


def conv_kernel(taps_ref, v_ref, cg_ref, above_ref, below_ref, conv_ref, back_ref, vp, cp):
    documents, tokens, channels = v_ref.shape
    taps = taps_ref.shape[0]
    rim = taps // 2
    for doc in range(documents):
        vp[doc, rim : rim + tokens, :] = v_ref[doc].astype(f32)
        cp[doc, rim : rim + tokens, :] = cg_ref[doc]
        for ref, start in ((above_ref, 0), (below_ref, rim + tokens)):
            rows = [ref[doc, i * rim : (i + 1) * rim, :].astype(f32) for i in range(3)]
            vp[doc, start : start + rim, :] = rows[0]
            cp[doc, start : start + rim, :] = rows[1] + rows[2]
    lane = lax.broadcasted_iota(jnp.int32, (1, channels), 1)
    for doc in range(documents):
        conv = jnp.zeros((tokens, channels), f32)
        back = jnp.zeros((tokens, channels), f32)
        for tap in range(taps):
            weight = jnp.where(lane < channels // 2, taps_ref[tap, 0], taps_ref[tap, 1])
            conv = conv + weight * vp[doc, tap : tap + tokens, :]
            start = 2 * rim - tap
            back = back + weight * cp[doc, start : start + tokens, :]
        conv_ref[doc] = conv
        back_ref[doc] = back


def context_kernel(got_ref, t_ref, inv_ref, conv_ref, ctx_ref, mixed_ref, mix_ref, lm_ref):
    documents, tokens, _ = conv_ref.shape
    groups = got_ref.shape[0] // 8
    for doc in range(documents):
        mixed = marks(got_ref, doc * SEGS, groups, 8)
        mixed_ref[doc] = mixed
        mix_ref[doc] = marks(got_ref, 4 + doc * SEGS, groups, 8)
        inverse = jnp.concatenate([inv_ref[doc * 2], inv_ref[doc * 2 + 1]], axis=0)
        landmark = own_blocks(prod(inverse, mixed))
        lm_ref[doc] = landmark
        ctx = (prod(t_ref[doc], landmark) + conv_ref[doc]).astype(bf16)
        ctx_ref[doc * tokens : (doc + 1) * tokens, :] = ctx


def main_kernel(
    scale, log_ref, t_ref, s_ref, cg_ref, qm_ref, km_ref, inv_ref, q_ref, k_ref, v_ref,
    back_ref, ogt_ref, ctx_ref, mixed_ref, mix_ref, lm_ref, out_ref, qd_ref, kd_ref, vg_ref, held,
):
    documents, tokens, channels = q_ref.shape
    count = qm_ref.shape[1]
    groups = count // SEGS
    for doc in range(documents):
        mixed = mixed_ref[doc]
        weights = t_ref[doc]
        upstream = prod(cg_ref[doc], lm_ref[doc], NT)
        back = weights * upstream
        back = jnp.concatenate(
            [
                back[:, part] - weights[:, part] * jnp.sum(back[:, part], axis=1, keepdims=True)
                for part in (slice(0, count), slice(count, 2 * count))
            ],
            axis=1,
        ) * scale
        qd_ref[doc] = prod(back, stack(km_ref[doc]))
        key_terms = pick(prod(back.T, q_ref[doc]))
        turned = jnp.concatenate([inv_ref[doc * 2].T, inv_ref[doc * 2 + 1].T], axis=0)
        mixed_grad = own_blocks(prod(turned, mix_ref[doc]))
        ones = jnp.ones((8, channels), bf16)
        mixed_dot = prod(ones, mixed_grad * stack(mixed), NT)[0:1]
        mixed_grad = halves(mixed_grad)
        log = jnp.concatenate(
            [log_ref[doc * 2 : doc * 2 + 1, :], log_ref[doc * 2 + 1 : doc * 2 + 2, :]], axis=1
        )
        key_weights = jnp.exp(s_ref[doc] - log)
        key_back = key_weights * (prod(v_ref[doc], mixed_grad, NT) - mixed_dot) * scale
        query_terms = pick(prod(key_back.T, k_ref[doc]))
        kd_ref[doc] = prod(key_back, stack(qm_ref[doc]))
        vg_ref[doc] = (prod(key_weights, mixed_grad) + back_ref[doc]).astype(bf16)
        for base, terms in ((0, query_terms), (4, key_terms)):
            high = terms.astype(bf16).astype(f32)
            low = terms - high
            for seg in range(SEGS):
                row = base + doc * SEGS + seg
                rows = slice(seg * groups, (seg + 1) * groups)
                held[pl.ds(row, groups, stride=16), :] = high[rows]
                held[pl.ds(8 + row, groups, stride=16), :] = low[rows]
    out_ref[:, 0:16, :] = held[...].astype(bf16).reshape(groups, 16, channels)
    terms = dot(ogt_ref[...], ctx_ref[...]).astype(bf16)
    out_ref[:, 16:, :] = terms.reshape(groups, terms.shape[0] // groups, channels)


def newton_back_kernel(scale, qm_ref, km_ref, mixed_ref, mix_ref, out_ref, held, *kept):
    documents, count, channels = qm_ref.shape
    me = lax.axis_index("seq")
    groups = count // SEGS
    every = range(documents * 2)
    units = landmark_units(scale, qm_ref, km_ref)
    newton(units, Kept(kept))
    approx_t, product_t, first_t, second_t, third_t = kept
    down = []
    for doc in range(documents):
        full = prod(stack(mix_ref[doc]), mixed_ref[doc], NT)
        down += [full[:count], full[count:]]
    unit_t = [halves(units[i].T) for i in every]
    grads = [None for i in every]
    for step in reversed(range(ITERS)):
        down = [halves(0.25 * down[i]) for i in every]
        turned = [halves(approx_t[step, i]) for i in every]
        product = [halves(product_t[step, i]) for i in every]
        third = [prod(turned[i], down[i]) for i in every]
        third = [halves(third[i]) for i in every]
        carry = [prod(down[i], third_t[step, i]) for i in every]
        second = [-prod(product[i], third[i]) for i in every]
        second = [halves(second[i]) for i in every]
        first = [-prod(product[i], second[i]) for i in every]
        flow = [
            -first[i] - prod(third[i], second_t[step, i]) - prod(second[i], first_t[step, i])
            for i in every
        ]
        flow = [halves(flow[i]) for i in every]
        more = [prod(flow[i], turned[i]) for i in every]
        grads = [more[i] if grads[i] is None else grads[i] + more[i] for i in every]
        down = [carry[i] + prod(unit_t[i], flow[i]) for i in every]
    for doc in range(documents):
        back, turned = [], []
        for head in range(2):
            i = doc * 2 + head
            unit = units[i]
            grad = grads[i] + down[i].T / column_peak(unit)
            part = unit * grad
            part = (part - unit * jnp.sum(part, axis=1, keepdims=True)) * scale
            back.append(part)
            turned.append(part.T)
        held[doc] = pick(prod(jnp.concatenate(back, axis=0), km_ref[doc]))
        held[documents + doc] = pick(prod(jnp.concatenate(turned, axis=0), qm_ref[doc]))
    for kind in range(2 * documents):
        for seg in range(SEGS):
            out_row = kind * SEGS + seg
            out_ref[out_row : out_row + 1, :] = held[kind, pl.ds(seg * groups + me, 1), :]


def finish_kernel(got_ref, own_ref, qd_ref, kd_ref, qg_ref, kg_ref, wg_ref):
    documents, tokens, _ = qd_ref.shape
    segment = tokens // SEGS
    total = jnp.sum(got_ref[:, 0:16, :].astype(f32), axis=0)
    total = (total[0:8] + total[8:16] + own_ref[...]) * (1.0 / segment)
    for base, source, target in ((0, qd_ref, qg_ref), (4, kd_ref, kg_ref)):
        for doc in range(documents):
            for seg in range(SEGS):
                row = base + doc * SEGS + seg
                rows = slice(seg * segment, (seg + 1) * segment)
                target[doc, rows, :] = (source[doc, rows, :] + total[row : row + 1]).astype(bf16)
    wg_ref[...] = jnp.sum(got_ref[:, 16:, :].astype(f32), axis=0)


def output_kernel(blocks, weights, *refs):
    total = None
    tokens = refs[-1].shape[0]
    for (index, block), (source, slot) in zip(blocks, weights):
        part = dot(refs[index][block * tokens : (block + 1) * tokens, :], refs[source][slot])
        total = part if total is None else total + part
    refs[-1][...] = total.astype(bf16)


def call(kernel, outs, *operands, scratch=(), smem=(), flops=1e8, size=2e6):
    vmem = pl.BlockSpec(memory_space=pltpu.VMEM)
    scalar = pl.BlockSpec(memory_space=pltpu.SMEM)
    return pl.pallas_call(
        kernel,
        out_shape=[jax.ShapeDtypeStruct(shape, kind) for shape, kind in outs],
        in_specs=[scalar if i in smem else vmem for i in range(len(operands))],
        out_specs=[vmem for _ in outs],
        scratch_shapes=list(scratch),
        compiler_params=pltpu.CompilerParams(vmem_limit_bytes=16 * 1024 * 1024),
        cost_estimate=pl.CostEstimate(
            flops=int(flops), bytes_accessed=int(size), transcendentals=0
        ),
    )(*operands)


def exchange(blocks, axis):
    return lax.all_to_all(blocks, axis, 0, 0, tiled=True)


def shift_by(block, shift, parts):
    pairs = []
    for i in range(lax.axis_size("seq")):
        step = shift if i % 2 == 0 else parts - shift
        pairs += [(i * parts + j, i * parts + (j + step) % parts) for j in range(parts)]
    return lax.ppermute(block, ("seq", "head"), pairs)


def gathered(block, parts):
    two, back_two = shift_by(block, 2, parts), shift_by(block, parts - 2, parts)
    one, back_one = shift_by(block, 1, parts), shift_by(block, parts - 1, parts)
    three, back_three = shift_by(two, 1, parts), shift_by(back_two, parts - 1, parts)
    return [block, one, two, three, shift_by(two, 2, parts), back_three, back_two, back_one]


def shards(queries, key_vectors, value_vectors, conv_taps, out_weight, out_grad):
    documents, tokens, channels = queries.shape
    heads = conv_taps.shape[1]
    groups = lax.axis_size("seq")
    parts = lax.axis_size("head")
    count = SEGS * groups
    scale = (channels // heads) ** (-0.5)
    rim = conv_taps.shape[0] // 2
    model_width = out_weight.shape[1]
    own_width = model_width // parts
    column_rows = model_width // groups
    rows_shape = (documents, tokens, channels)
    marks_shape = (documents, count, channels)
    pair_shape = (documents, tokens, 2 * count)
    units = 2 * documents
    saved = (ITERS, units, count, count)

    (sent,) = call(means_kernel, [((groups, 8, channels), f32)], queries, key_vectors)
    own_grad, sent = lax.optimization_barrier((out_grad, sent))
    got = exchange(sent, "seq").reshape(groups * 8, channels)
    og_parts = gathered(own_grad.reshape(documents * tokens, own_width), parts)

    weights, scores, local_mixed, local_log, qm, km = call(
        functools.partial(stats_kernel, scale),
        [
            (pair_shape, f32),
            (pair_shape, f32),
            (marks_shape, f32),
            ((8, count), f32),
            (marks_shape, f32),
            (marks_shape, f32),
        ],
        got, queries, key_vectors, value_vectors,
    )
    (inverse,) = call(
        functools.partial(inverse_kernel, scale), [((units, count, count), f32)], qm, km, flops=2e9
    )
    og_parts, inverse = lax.optimization_barrier((og_parts, inverse))
    sent, context_grad, first_rows, last_rows, *pieces = call(
        functools.partial(chunk_kernel, parts, rim),
        [((groups * 16, channels), f32), (rows_shape, f32)]
        + [((documents, 3 * rim, channels), bf16)] * 2
        + [((len(shifts), channels, own_width), bf16) for shifts in PIECES],
        *og_parts, out_weight, value_vectors, weights, local_mixed, local_log,
    )
    got = exchange(sent, "seq")
    ends = groups - 1
    above = lax.ppermute(last_rows, "seq", [(i, i + 1) for i in range(ends)])
    below = lax.ppermute(first_rows, "seq", [(i + 1, i) for i in range(ends)])
    kept, stay, up, down, across = pieces
    up = shift_by(up, 1, parts)
    down = shift_by(down, parts - 1, parts)
    across = shift_by(across, 4, parts)
    got, up, down, across, above, below = lax.optimization_barrier(
        (got, up, down, across, above, below)
    )
    sent, logs = call(
        combine_kernel, [((groups, 8, channels), f32), ((8, count), f32)], got
    )
    sent, up, down, stay, og_parts = lax.optimization_barrier((sent, up, down, stay, og_parts))
    (og_turned,) = call(
        functools.partial(turn_kernel, parts), [((model_width, documents * tokens), bf16)], *og_parts
    )
    got = exchange(sent, "seq").reshape(groups * 8, channels)
    conv, back = call(
        conv_kernel,
        [(rows_shape, f32), (rows_shape, f32)],
        conv_taps, value_vectors, context_grad, above, below,
        scratch=[pltpu.VMEM((documents, tokens + 2 * rim, channels), f32)] * 2,
        smem=(0,),
        flops=1e9,
    )
    up_two = shift_by(jnp.concatenate([stay[0:1], up[1:2]], axis=0), 2, parts)
    down_two = shift_by(jnp.concatenate([stay[1:2], down[1:2]], axis=0), parts - 2, parts)
    got, up_two, down_two, conv, back, og_turned = lax.optimization_barrier(
        (got, up_two, down_two, conv, back, og_turned)
    )
    weight_parts = [kept, up, down, across, up_two, down_two]
    context_b, mixed, mix, landmark_mix = call(
        context_kernel,
        [
            ((documents * tokens, channels), bf16),
            (marks_shape, f32),
            (marks_shape, f32),
            ((documents, 2 * count, channels), f32),
        ],
        got, weights, inverse, conv,
    )
    near = [shift_by(context_b, 1, parts), shift_by(context_b, parts - 1, parts)]
    sent, query_direct, key_direct, value_grad = call(
        functools.partial(main_kernel, scale),
        [
            ((groups, 16 + column_rows, channels), bf16),
            (rows_shape, f32),
            (rows_shape, f32),
            (rows_shape, bf16),
        ],
        logs, weights, scores, context_grad, qm, km, inverse, queries, key_vectors,
        value_vectors, back, og_turned, context_b, mixed, mix, landmark_mix,
        scratch=[pltpu.VMEM((groups * 16, channels), f32)],
        flops=1e9,
    )
    sent, near, mix = lax.optimization_barrier((sent, near, mix))
    got = exchange(sent, "seq")
    far = [
        shift_by(jnp.concatenate([near[0], context_b, near[1]], axis=0), 3, parts),
        shift_by(jnp.concatenate([near[0], context_b], axis=0), parts - 3, parts),
    ]
    (own,) = call(
        functools.partial(newton_back_kernel, scale),
        [((8, channels), f32)],
        qm, km, mixed, mix,
        scratch=[pltpu.VMEM((2 * documents, count, channels), f32)] + [pltpu.VMEM(saved, f32)] * 5,
        flops=5e9,
    )
    blocks = ((0, 0), (1, 0), (3, 2), (3, 1), (3, 0), (4, 1), (4, 0), (2, 0))
    slots = ((5, 0), (6, 0), (9, 0), (9, 1), (8, 0), (10, 1), (10, 0), (7, 0))
    (layer_output,) = call(
        functools.partial(output_kernel, blocks, slots),
        [((documents * tokens, own_width), bf16)],
        context_b, *near, *far, *weight_parts,
    )
    query_grad, key_grad, weight_grad = call(
        finish_kernel,
        [(rows_shape, bf16), (rows_shape, bf16), ((column_rows, channels), f32)],
        got, own, query_direct, key_direct,
    )
    return (
        layer_output.reshape(documents, tokens, own_width),
        query_grad,
        key_grad,
        value_grad,
        weight_grad.T,
    )


def solution(mesh):
    in_specs = (
        P(None, "seq", "head"),
        P(None, "seq", "head"),
        P(None, "seq", "head"),
        P(None, "head"),
        P("head", None),
        P(None, "seq", "head"),
    )
    out_specs = (
        P(None, "seq", "head"),
        P(None, "seq", "head"),
        P(None, "seq", "head"),
        P(None, "seq", "head"),
        P("head", "seq"),
    )
    return jax.shard_map(shards, mesh=mesh, in_specs=in_specs, out_specs=out_specs, check_vma=False)
```

```python
import functools

import jax
import jax.numpy as jnp
from jax import lax
from jax.experimental import pallas as pl
from jax.experimental.pallas import tpu as pltpu
from jax.sharding import PartitionSpec as P

ITERS = 2
SEGS = 2
f32 = jnp.float32
bf16 = jnp.bfloat16
NN = (((1,), (0,)), ((), ()))
NT = (((1,), (1,)), ((), ()))


def dot(left, right, dims=NN):
    return lax.dot_general(left, right, dims, preferred_element_type=f32)


def halves(value):
    if value.dtype == bf16:
        return (value,)
    high = value.astype(bf16)
    return high, (value - high.astype(f32)).astype(bf16)


def prod(left, right, dims=NN):
    left = left if isinstance(left, tuple) else halves(left)
    right = right if isinstance(right, tuple) else halves(right)
    total = dot(left[0], right[0], dims)
    if len(right) > 1:
        total = total + dot(left[0], right[1], dims)
    if len(left) > 1:
        total = total + dot(left[1], right[0], dims)
    return total


def block_at(shift, parts):
    core = lax.rem(lax.axis_index("seq"), 2)
    step = jnp.where(core == 0, parts - shift, parts + shift)
    return lax.rem(lax.axis_index("head") + step, parts)


def first_head(shape):
    return lax.broadcasted_iota(jnp.int32, shape, 1) < shape[1] // 2


def stack(rows):
    mask = first_head(rows.shape)
    zero = jnp.zeros_like(rows)
    return jnp.concatenate([jnp.where(mask, rows, zero), jnp.where(mask, zero, rows)], axis=0)


def own_blocks(full):
    count = full.shape[0] // 2
    mask = first_head((count, full.shape[1]))
    zero = jnp.zeros((count, full.shape[1]), full.dtype)
    return jnp.concatenate(
        [jnp.where(mask, full[:count], zero), jnp.where(mask, zero, full[count:])], axis=0
    )


def pick(full):
    count = full.shape[0] // 2
    return jnp.where(first_head((count, full.shape[1])), full[:count], full[count:])


def marks(ref, row, groups, stride):
    return jnp.concatenate(
        [ref[pl.ds(row + seg, groups, stride=stride), :] for seg in range(SEGS)], axis=0
    )


def means_kernel(q_ref, k_ref, out_ref):
    documents, tokens, _ = q_ref.shape
    segment = tokens // SEGS
    rows = []
    for ref in (q_ref, k_ref):
        for doc in range(documents):
            for seg in range(SEGS):
                part = ref[doc, seg * segment : (seg + 1) * segment, :].astype(f32)
                rows.append(jnp.sum(part, axis=0, keepdims=True) * (1.0 / segment))
    block = jnp.concatenate(rows, axis=0)
    out_ref[...] = jnp.broadcast_to(block[None], out_ref.shape)


def stats_kernel(scale, got_ref, q_ref, k_ref, v_ref, t_ref, s_ref, o_ref, log_ref, qm_ref, km_ref):
    documents = q_ref.shape[0]
    groups = got_ref.shape[0] // 8
    count = SEGS * groups
    logs = []
    for doc in range(documents):
        qm = marks(got_ref, doc * SEGS, groups, 8)
        km = marks(got_ref, 4 + doc * SEGS, groups, 8)
        qm_ref[doc] = qm
        km_ref[doc] = km
        scores = prod(q_ref[doc], stack(km), NT) * scale
        for head in range(2):
            part = scores[:, head * count : (head + 1) * count]
            part = jnp.exp(part - jnp.max(part, axis=1, keepdims=True))
            t_ref[doc, :, head * count : (head + 1) * count] = part / jnp.sum(
                part, axis=1, keepdims=True
            )
        scores = prod(k_ref[doc], stack(qm), NT) * scale
        s_ref[doc] = scores
        peak = jnp.max(scores, axis=0, keepdims=True)
        part = jnp.exp(scores - peak)
        total = jnp.sum(part, axis=0, keepdims=True)
        o_ref[doc] = pick(prod((part / total).T, v_ref[doc]))
        log = peak + jnp.log(total)
        logs += [log[:, :count], log[:, count:]]
    logs.append(jnp.zeros((8 - len(logs), count), f32))
    log_ref[...] = jnp.concatenate(logs, axis=0)


def pack_kernel(parts, og_ref, w_ref, up_ref, down_ref, up_two_ref, down_two_ref, kept_ref):
    width = og_ref.shape[1]
    for ref, items in (
        (up_ref, (None, 1)),
        (down_ref, (None, 7)),
        (up_two_ref, (4, None, 3, 2)),
        (down_two_ref, (None, 5, 6)),
        (kept_ref, (0,)),
    ):
        row = 0
        for shift in items:
            if shift is None:
                block = og_ref[...]
            else:
                start = pl.multiple_of(block_at(-shift, parts) * width, width)
                block = w_ref[:, pl.ds(start, width)]
            ref[row : row + block.shape[0], :] = block
            row += block.shape[0]


def chunk_kernel(parts, rim, starts, *refs):
    og_refs = refs[:parts]
    w_ref, v_ref, t_ref, o_ref, log_ref = refs[parts : parts + 5]
    out_ref, cg_ref, head_ref, tail_ref = refs[parts + 5 :]
    documents, tokens, channels = cg_ref.shape
    groups = out_ref.shape[0] // 16
    width = w_ref.shape[1] // parts

    def columns(shift):
        return pl.ds(pl.multiple_of(block_at(shift, parts) * width, width), width)

    total = None
    for shift in range(parts):
        block = og_refs[shift][starts[shift] : starts[shift] + documents * tokens, :]
        part = dot(block, w_ref[:, columns(shift)], NT)
        total = part if total is None else total + part
    for doc in range(documents):
        grad = total[doc * tokens : (doc + 1) * tokens]
        cg_ref[doc] = grad
        for ref, rows in ((head_ref, slice(0, rim)), (tail_ref, slice(tokens - rim, tokens))):
            high, low = halves(grad[rows])
            ref[doc, 0:rim, :] = v_ref[doc, rows, :]
            ref[doc, rim : 2 * rim, :] = high
            ref[doc, 2 * rim : 3 * rim, :] = low
        mix = pick(prod(t_ref[doc].T, grad))
        for seg in range(SEGS):
            row = doc * SEGS + seg
            rows = slice(seg * groups, (seg + 1) * groups)
            out_ref[pl.ds(row, groups, stride=16), :] = o_ref[doc, rows, :]
            out_ref[pl.ds(4 + row, groups, stride=16), :] = mix[rows]
    for row in range(8):
        out_ref[pl.ds(8 + row, groups, stride=16), :] = jnp.broadcast_to(
            log_ref[row : row + 1, :], (groups, channels)
        )


def landmark_units(scale, qm_ref, km_ref):
    count = qm_ref.shape[1]
    units = []
    for doc in range(qm_ref.shape[0]):
        scores = prod(stack(qm_ref[doc]), km_ref[doc], NT) * scale
        scores = jnp.exp(scores - jnp.max(scores, axis=1, keepdims=True))
        scores = scores / jnp.sum(scores, axis=1, keepdims=True)
        units += [scores[:count], scores[count:]]
    return units


def column_peak(unit):
    return jnp.max(jnp.sum(unit, axis=0, keepdims=True), axis=1, keepdims=True)


def newton(units, keep):
    every = range(len(units))
    count = units[0].shape[0]
    row = lax.broadcasted_iota(jnp.int32, (count, count), 0)
    identity = (row == lax.broadcasted_iota(jnp.int32, (count, count), 1)).astype(f32)
    approx = [unit.T / column_peak(unit) for unit in units]
    units = [halves(unit) for unit in units]
    for step in range(ITERS):
        spread = [halves(approx[i]) for i in every]
        product = [prod(units[i], spread[i]) for i in every]
        first = [7.0 * identity - product[i] for i in every]
        split = [halves(product[i]) for i in every]
        second = [15.0 * identity - prod(split[i], first[i]) for i in every]
        third = [13.0 * identity - prod(split[i], second[i]) for i in every]
        for i in every:
            keep(step, i, (approx[i], product[i], first[i], second[i], third[i]))
        if step < ITERS - 1 or not keep.last:
            approx = [0.25 * prod(spread[i], third[i]) for i in every]
    return approx


class Nothing:
    last = False

    def __call__(self, step, index, values):
        pass


class Kept:
    last = True

    def __init__(self, refs):
        self.refs = refs

    def __call__(self, step, index, values):
        for ref, value in zip(self.refs, values):
            ref[step, index] = value.T


def inverse_kernel(scale, qm_ref, km_ref, inv_ref):
    for index, unit in enumerate(newton(landmark_units(scale, qm_ref, km_ref), Nothing())):
        inv_ref[index] = unit


def turn_kernel(parts, starts, *refs):
    count, width = refs[parts].shape[1], refs[0].shape[1]
    for shift in range(parts):
        start = pl.multiple_of(block_at(shift, parts) * width, width)
        refs[parts][pl.ds(start, width), :] = refs[shift][starts[shift] : starts[shift] + count, :].T


def combine_kernel(got_ref, out_ref, log_ref):
    groups = got_ref.shape[0] // 16
    channels = got_ref.shape[1]
    me = lax.axis_index("seq")
    lane = lax.broadcasted_iota(jnp.int32, (groups, channels), 1)
    shares, logs = [], []
    for unit in range(4):
        log = got_ref[pl.ds(8 + unit, groups, stride=16), :]
        top = jnp.max(log, axis=0, keepdims=True)
        part = jnp.exp(log - top)
        total = jnp.sum(part, axis=0, keepdims=True)
        logs.append(top + jnp.log(total))
        shares.append(part / total)
    logs.append(jnp.zeros((4, channels), f32))
    log_ref[...] = jnp.concatenate(logs, axis=0)
    mixed, mix = [], []
    for doc in range(2):
        for seg in range(SEGS):
            row = doc * SEGS + seg
            weight = [
                jnp.sum(
                    jnp.where(lane == seg * groups + me, shares[doc * 2 + head], 0.0),
                    axis=1,
                    keepdims=True,
                )
                for head in range(2)
            ]
            weight = jnp.where(lane < channels // 2, weight[0], weight[1])
            mixed.append(
                jnp.sum(weight * got_ref[pl.ds(row, groups, stride=16), :], axis=0, keepdims=True)
            )
            mix.append(jnp.sum(got_ref[pl.ds(4 + row, groups, stride=16), :], axis=0, keepdims=True))
    block = jnp.concatenate(mixed + mix, axis=0)
    out_ref[...] = jnp.broadcast_to(block[None], out_ref.shape)


def conv_kernel(taps_ref, v_ref, cg_ref, above_ref, below_ref, conv_ref, back_ref, vp, cp):
    documents, tokens, channels = v_ref.shape
    taps = taps_ref.shape[0]
    rim = taps // 2
    for doc in range(documents):
        vp[doc, rim : rim + tokens, :] = v_ref[doc].astype(f32)
        cp[doc, rim : rim + tokens, :] = cg_ref[doc]
        for ref, start in ((above_ref, 0), (below_ref, rim + tokens)):
            rows = [ref[doc, i * rim : (i + 1) * rim, :].astype(f32) for i in range(3)]
            vp[doc, start : start + rim, :] = rows[0]
            cp[doc, start : start + rim, :] = rows[1] + rows[2]
    lane = lax.broadcasted_iota(jnp.int32, (1, channels), 1)
    for doc in range(documents):
        conv = jnp.zeros((tokens, channels), f32)
        back = jnp.zeros((tokens, channels), f32)
        for tap in range(taps):
            weight = jnp.where(lane < channels // 2, taps_ref[tap, 0], taps_ref[tap, 1])
            conv = conv + weight * vp[doc, tap : tap + tokens, :]
            start = 2 * rim - tap
            back = back + weight * cp[doc, start : start + tokens, :]
        conv_ref[doc] = conv
        back_ref[doc] = back


def context_kernel(got_ref, t_ref, inv_ref, conv_ref, ctx_ref, mixed_ref, mix_ref, lm_ref):
    documents, tokens, _ = conv_ref.shape
    groups = got_ref.shape[0] // 8
    for doc in range(documents):
        mixed = marks(got_ref, doc * SEGS, groups, 8)
        mixed_ref[doc] = mixed
        mix_ref[doc] = marks(got_ref, 4 + doc * SEGS, groups, 8)
        inverse = jnp.concatenate([inv_ref[doc * 2], inv_ref[doc * 2 + 1]], axis=0)
        landmark = own_blocks(prod(inverse, mixed))
        lm_ref[doc] = landmark
        ctx = (prod(t_ref[doc], landmark) + conv_ref[doc]).astype(bf16)
        ctx_ref[doc * tokens : (doc + 1) * tokens, :] = ctx


def main_kernel(
    scale, log_ref, t_ref, s_ref, cg_ref, qm_ref, km_ref, inv_ref, q_ref, k_ref, v_ref,
    back_ref, ogt_ref, ctx_ref, mixed_ref, mix_ref, lm_ref, out_ref, qd_ref, kd_ref, vg_ref, held,
):
    documents, tokens, channels = q_ref.shape
    count = qm_ref.shape[1]
    groups = count // SEGS
    for doc in range(documents):
        mixed = mixed_ref[doc]
        weights = t_ref[doc]
        upstream = prod(cg_ref[doc], lm_ref[doc], NT)
        back = weights * upstream
        back = jnp.concatenate(
            [
                back[:, part] - weights[:, part] * jnp.sum(back[:, part], axis=1, keepdims=True)
                for part in (slice(0, count), slice(count, 2 * count))
            ],
            axis=1,
        ) * scale
        qd_ref[doc] = prod(back, stack(km_ref[doc]))
        key_terms = pick(prod(back.T, q_ref[doc]))
        turned = jnp.concatenate([inv_ref[doc * 2].T, inv_ref[doc * 2 + 1].T], axis=0)
        mixed_grad = own_blocks(prod(turned, mix_ref[doc]))
        ones = jnp.ones((8, channels), bf16)
        mixed_dot = prod(ones, mixed_grad * stack(mixed), NT)[0:1]
        mixed_grad = halves(mixed_grad)
        log = jnp.concatenate(
            [log_ref[doc * 2 : doc * 2 + 1, :], log_ref[doc * 2 + 1 : doc * 2 + 2, :]], axis=1
        )
        key_weights = jnp.exp(s_ref[doc] - log)
        key_back = key_weights * (prod(v_ref[doc], mixed_grad, NT) - mixed_dot) * scale
        query_terms = pick(prod(key_back.T, k_ref[doc]))
        kd_ref[doc] = prod(key_back, stack(qm_ref[doc]))
        vg_ref[doc] = (prod(key_weights, mixed_grad) + back_ref[doc]).astype(bf16)
        for base, terms in ((0, query_terms), (4, key_terms)):
            high = terms.astype(bf16).astype(f32)
            low = terms - high
            for seg in range(SEGS):
                row = base + doc * SEGS + seg
                rows = slice(seg * groups, (seg + 1) * groups)
                held[pl.ds(row, groups, stride=16), :] = high[rows]
                held[pl.ds(8 + row, groups, stride=16), :] = low[rows]
    out_ref[:, 0:16, :] = held[...].astype(bf16).reshape(groups, 16, channels)
    terms = dot(ogt_ref[...], ctx_ref[...]).astype(bf16)
    out_ref[:, 16:, :] = terms.reshape(groups, terms.shape[0] // groups, channels)


def newton_back_kernel(scale, qm_ref, km_ref, mixed_ref, mix_ref, out_ref, held, *kept):
    documents, count, channels = qm_ref.shape
    me = lax.axis_index("seq")
    groups = count // SEGS
    every = range(documents * 2)
    units = landmark_units(scale, qm_ref, km_ref)
    newton(units, Kept(kept))
    approx_t, product_t, first_t, second_t, third_t = kept
    down = []
    for doc in range(documents):
        full = prod(stack(mix_ref[doc]), mixed_ref[doc], NT)
        down += [full[:count], full[count:]]
    unit_t = [halves(units[i].T) for i in every]
    grads = [None for i in every]
    for step in reversed(range(ITERS)):
        down = [halves(0.25 * down[i]) for i in every]
        turned = [halves(approx_t[step, i]) for i in every]
        product = [halves(product_t[step, i]) for i in every]
        third = [prod(turned[i], down[i]) for i in every]
        third = [halves(third[i]) for i in every]
        carry = [prod(down[i], third_t[step, i]) for i in every]
        second = [-prod(product[i], third[i]) for i in every]
        second = [halves(second[i]) for i in every]
        first = [-prod(product[i], second[i]) for i in every]
        flow = [
            -first[i] - prod(third[i], second_t[step, i]) - prod(second[i], first_t[step, i])
            for i in every
        ]
        flow = [halves(flow[i]) for i in every]
        more = [prod(flow[i], turned[i]) for i in every]
        grads = [more[i] if grads[i] is None else grads[i] + more[i] for i in every]
        down = [carry[i] + prod(unit_t[i], flow[i]) for i in every]
    for doc in range(documents):
        back, turned = [], []
        for head in range(2):
            i = doc * 2 + head
            unit = units[i]
            grad = grads[i] + down[i].T / column_peak(unit)
            part = unit * grad
            part = (part - unit * jnp.sum(part, axis=1, keepdims=True)) * scale
            back.append(part)
            turned.append(part.T)
        held[doc] = pick(prod(jnp.concatenate(back, axis=0), km_ref[doc]))
        held[documents + doc] = pick(prod(jnp.concatenate(turned, axis=0), qm_ref[doc]))
    for kind in range(2 * documents):
        for seg in range(SEGS):
            out_row = kind * SEGS + seg
            out_ref[out_row : out_row + 1, :] = held[kind, pl.ds(seg * groups + me, 1), :]


def finish_kernel(got_ref, own_ref, qd_ref, kd_ref, qg_ref, kg_ref, wg_ref):
    documents, tokens, _ = qd_ref.shape
    segment = tokens // SEGS
    total = jnp.sum(got_ref[:, 0:16, :].astype(f32), axis=0)
    total = (total[0:8] + total[8:16] + own_ref[...]) * (1.0 / segment)
    for base, source, target in ((0, qd_ref, qg_ref), (4, kd_ref, kg_ref)):
        for doc in range(documents):
            for seg in range(SEGS):
                row = base + doc * SEGS + seg
                rows = slice(seg * segment, (seg + 1) * segment)
                target[doc, rows, :] = (source[doc, rows, :] + total[row : row + 1]).astype(bf16)
    wg_ref[...] = jnp.sum(got_ref[:, 16:, :].astype(f32), axis=0)


def output_kernel(blocks, weights, *refs):
    total = None
    tokens = refs[-1].shape[0]
    channels = refs[0].shape[1]
    for (index, block), (source, row) in zip(blocks, weights):
        weight = refs[source][row : row + channels, :]
        part = dot(refs[index][block * tokens : (block + 1) * tokens, :], weight)
        total = part if total is None else total + part
    refs[-1][...] = total.astype(bf16)


def call(kernel, outs, *operands, scratch=(), smem=(), flops=1e8, size=2e6):
    vmem = pl.BlockSpec(memory_space=pltpu.VMEM)
    scalar = pl.BlockSpec(memory_space=pltpu.SMEM)
    return pl.pallas_call(
        kernel,
        out_shape=[jax.ShapeDtypeStruct(shape, kind) for shape, kind in outs],
        in_specs=[scalar if i in smem else vmem for i in range(len(operands))],
        out_specs=[vmem for _ in outs],
        scratch_shapes=list(scratch),
        compiler_params=pltpu.CompilerParams(vmem_limit_bytes=16 * 1024 * 1024),
        cost_estimate=pl.CostEstimate(
            flops=int(flops), bytes_accessed=int(size), transcendentals=0
        ),
    )(*operands)


def exchange(blocks, axis):
    return lax.all_to_all(blocks, axis, 0, 0, tiled=True)


def shift_by(block, shift, parts):
    pairs = []
    for i in range(lax.axis_size("seq")):
        step = shift if i % 2 == 0 else parts - shift
        pairs += [(i * parts + j, i * parts + (j + step) % parts) for j in range(parts)]
    return lax.ppermute(block, ("seq", "head"), pairs)


def shards(queries, key_vectors, value_vectors, conv_taps, out_weight, out_grad):
    documents, tokens, channels = queries.shape
    heads = conv_taps.shape[1]
    groups = lax.axis_size("seq")
    parts = lax.axis_size("head")
    count = SEGS * groups
    scale = (channels // heads) ** (-0.5)
    rim = conv_taps.shape[0] // 2
    model_width = out_weight.shape[1]
    own_width = model_width // parts
    column_rows = model_width // groups
    rows_shape = (documents, tokens, channels)
    marks_shape = (documents, count, channels)
    pair_shape = (documents, tokens, 2 * count)
    units = 2 * documents
    saved = (ITERS, units, count, count)

    (sent,) = call(means_kernel, [((groups, 8, channels), f32)], queries, key_vectors)
    own_grad, sent = lax.optimization_barrier((out_grad, sent))
    got = exchange(sent, "seq").reshape(groups * 8, channels)
    own_grad = own_grad.reshape(documents * tokens, own_width)
    rows = documents * tokens
    up, down, up_two, down_two, kept = call(
        functools.partial(pack_kernel, parts),
        [((rows + pieces * channels, own_width), bf16) for pieces in (1, 1, 3, 2)]
        + [((channels, own_width), bf16)],
        own_grad, out_weight,
    )
    up_two, down_two = shift_by(up_two, 2, parts), shift_by(down_two, parts - 2, parts)
    up, down = shift_by(up, 1, parts), shift_by(down, parts - 1, parts)
    up_three = shift_by(up_two[channels : rows + 2 * channels], 1, parts)
    down_three = shift_by(down_two[: rows + channels], parts - 1, parts)
    across = shift_by(up_two[: rows + channels], 2, parts)
    og_parts = [own_grad, up, up_two, up_three, across, down_three, down_two, down]
    og_starts = (0, 0, channels, 0, channels, 0, 0, 0)
    w_starts = (0, rows, rows + 2 * channels, rows, 0, rows, rows + channels, rows)

    weights, scores, local_mixed, local_log, qm, km = call(
        functools.partial(stats_kernel, scale),
        [
            (pair_shape, f32),
            (pair_shape, f32),
            (marks_shape, f32),
            ((8, count), f32),
            (marks_shape, f32),
            (marks_shape, f32),
        ],
        got, queries, key_vectors, value_vectors,
    )
    sent, context_grad, first_rows, last_rows = call(
        functools.partial(chunk_kernel, parts, rim, og_starts),
        [((groups * 16, channels), f32), (rows_shape, f32)]
        + [((documents, 3 * rim, channels), bf16)] * 2,
        *og_parts, out_weight, value_vectors, weights, local_mixed, local_log,
    )
    sent, qm, km = lax.optimization_barrier((sent, qm, km))
    got = exchange(sent, "seq")
    ends = groups - 1
    above = lax.ppermute(last_rows, "seq", [(i, i + 1) for i in range(ends)])
    below = lax.ppermute(first_rows, "seq", [(i + 1, i) for i in range(ends)])
    (inverse,) = call(
        functools.partial(inverse_kernel, scale), [((units, count, count), f32)], qm, km, flops=2e9
    )
    got, above, below, inverse = lax.optimization_barrier((got, above, below, inverse))
    sent, logs = call(
        combine_kernel, [((groups, 8, channels), f32), ((8, count), f32)], got
    )
    sent, og_parts = lax.optimization_barrier((sent, og_parts))
    (og_turned,) = call(
        functools.partial(turn_kernel, parts, og_starts), [((model_width, documents * tokens), bf16)], *og_parts
    )
    got = exchange(sent, "seq").reshape(groups * 8, channels)
    conv, back = call(
        conv_kernel,
        [(rows_shape, f32), (rows_shape, f32)],
        conv_taps, value_vectors, context_grad, above, below,
        scratch=[pltpu.VMEM((documents, tokens + 2 * rim, channels), f32)] * 2,
        smem=(0,),
        flops=1e9,
    )
    got, conv, back, og_turned = lax.optimization_barrier((got, conv, back, og_turned))
    weight_parts = [kept] + og_parts[1:]
    context_b, mixed, mix, landmark_mix = call(
        context_kernel,
        [
            ((documents * tokens, channels), bf16),
            (marks_shape, f32),
            (marks_shape, f32),
            ((documents, 2 * count, channels), f32),
        ],
        got, weights, inverse, conv,
    )
    near = [shift_by(context_b, 1, parts), shift_by(context_b, parts - 1, parts)]
    sent, query_direct, key_direct, value_grad = call(
        functools.partial(main_kernel, scale),
        [
            ((groups, 16 + column_rows, channels), bf16),
            (rows_shape, f32),
            (rows_shape, f32),
            (rows_shape, bf16),
        ],
        logs, weights, scores, context_grad, qm, km, inverse, queries, key_vectors,
        value_vectors, back, og_turned, context_b, mixed, mix, landmark_mix,
        scratch=[pltpu.VMEM((groups * 16, channels), f32)],
        flops=1e9,
    )
    sent, near, mix = lax.optimization_barrier((sent, near, mix))
    got = exchange(sent, "seq")
    far = [
        shift_by(jnp.concatenate([near[0], context_b, near[1]], axis=0), 3, parts),
        shift_by(jnp.concatenate([near[0], context_b], axis=0), parts - 3, parts),
    ]
    (own,) = call(
        functools.partial(newton_back_kernel, scale),
        [((8, channels), f32)],
        qm, km, mixed, mix,
        scratch=[pltpu.VMEM((2 * documents, count, channels), f32)] + [pltpu.VMEM(saved, f32)] * 5,
        flops=5e9,
    )
    blocks = ((0, 0), (1, 0), (3, 2), (3, 1), (3, 0), (4, 1), (4, 0), (2, 0))
    slots = tuple((5 + shift, start) for shift, start in enumerate(w_starts))
    (layer_output,) = call(
        functools.partial(output_kernel, blocks, slots),
        [((documents * tokens, own_width), bf16)],
        context_b, *near, *far, *weight_parts,
    )
    query_grad, key_grad, weight_grad = call(
        finish_kernel,
        [(rows_shape, bf16), (rows_shape, bf16), ((column_rows, channels), f32)],
        got, own, query_direct, key_direct,
    )
    return (
        layer_output.reshape(documents, tokens, own_width),
        query_grad,
        key_grad,
        value_grad,
        weight_grad.T,
    )


def solution(mesh):
    in_specs = (
        P(None, "seq", "head"),
        P(None, "seq", "head"),
        P(None, "seq", "head"),
        P(None, "head"),
        P("head", None),
        P(None, "seq", "head"),
    )
    out_specs = (
        P(None, "seq", "head"),
        P(None, "seq", "head"),
        P(None, "seq", "head"),
        P(None, "seq", "head"),
        P("head", "seq"),
    )
    return jax.shard_map(shards, mesh=mesh, in_specs=in_specs, out_specs=out_specs, check_vma=False)
```

```python
import functools

import jax
import jax.numpy as jnp
from jax import lax
from jax.experimental import pallas as pl
from jax.experimental.pallas import tpu as pltpu
from jax.sharding import PartitionSpec as P

ITERS = 2
SEGS = 2
f32 = jnp.float32
bf16 = jnp.bfloat16
NN = (((1,), (0,)), ((), ()))
NT = (((1,), (1,)), ((), ()))


def dot(left, right, dims=NN):
    return lax.dot_general(left, right, dims, preferred_element_type=f32)


def halves(value):
    if value.dtype == bf16:
        return (value,)
    high = value.astype(bf16)
    return high, (value - high.astype(f32)).astype(bf16)


def prod(left, right, dims=NN):
    left = left if isinstance(left, tuple) else halves(left)
    right = right if isinstance(right, tuple) else halves(right)
    total = dot(left[0], right[0], dims)
    if len(right) > 1:
        total = total + dot(left[0], right[1], dims)
    if len(left) > 1:
        total = total + dot(left[1], right[0], dims)
    return total


def block_at(shift, parts):
    core = lax.rem(lax.axis_index("seq"), 2)
    step = jnp.where(core == 0, parts - shift, parts + shift)
    return lax.rem(lax.axis_index("head") + step, parts)


def first_head(shape):
    return lax.broadcasted_iota(jnp.int32, shape, 1) < shape[1] // 2


def stack(rows):
    mask = first_head(rows.shape)
    zero = jnp.zeros_like(rows)
    return jnp.concatenate([jnp.where(mask, rows, zero), jnp.where(mask, zero, rows)], axis=0)


def own_blocks(full):
    count = full.shape[0] // 2
    mask = first_head((count, full.shape[1]))
    zero = jnp.zeros((count, full.shape[1]), full.dtype)
    return jnp.concatenate(
        [jnp.where(mask, full[:count], zero), jnp.where(mask, zero, full[count:])], axis=0
    )


def pick(full):
    count = full.shape[0] // 2
    return jnp.where(first_head((count, full.shape[1])), full[:count], full[count:])


def marks(ref, row, groups, stride):
    return jnp.concatenate(
        [ref[pl.ds(row + seg, groups, stride=stride), :] for seg in range(SEGS)], axis=0
    )


def means_kernel(q_ref, k_ref, out_ref):
    documents, tokens, _ = q_ref.shape
    segment = tokens // SEGS
    rows = []
    for ref in (q_ref, k_ref):
        for doc in range(documents):
            for seg in range(SEGS):
                part = ref[doc, seg * segment : (seg + 1) * segment, :].astype(f32)
                rows.append(jnp.sum(part, axis=0, keepdims=True) * (1.0 / segment))
    block = jnp.concatenate(rows, axis=0)
    out_ref[...] = jnp.broadcast_to(block[None], out_ref.shape)


def stats_kernel(scale, got_ref, q_ref, k_ref, v_ref, t_ref, s_ref, o_ref, log_ref, qm_ref, km_ref):
    documents = q_ref.shape[0]
    groups = got_ref.shape[0] // 8
    count = SEGS * groups
    logs = []
    for doc in range(documents):
        qm = marks(got_ref, doc * SEGS, groups, 8)
        km = marks(got_ref, 4 + doc * SEGS, groups, 8)
        qm_ref[doc] = qm
        km_ref[doc] = km
        scores = prod(q_ref[doc], stack(km), NT) * scale
        for head in range(2):
            part = scores[:, head * count : (head + 1) * count]
            part = jnp.exp(part - jnp.max(part, axis=1, keepdims=True))
            t_ref[doc, :, head * count : (head + 1) * count] = part / jnp.sum(
                part, axis=1, keepdims=True
            )
        scores = prod(k_ref[doc], stack(qm), NT) * scale
        s_ref[doc] = scores
        peak = jnp.max(scores, axis=0, keepdims=True)
        part = jnp.exp(scores - peak)
        total = jnp.sum(part, axis=0, keepdims=True)
        o_ref[doc] = pick(prod((part / total).T, v_ref[doc]))
        log = peak + jnp.log(total)
        logs += [log[:, :count], log[:, count:]]
    logs.append(jnp.zeros((8 - len(logs), count), f32))
    log_ref[...] = jnp.concatenate(logs, axis=0)


def pack_kernel(parts, og_ref, w_ref, up_ref, down_ref, up_two_ref, down_two_ref, kept_ref):
    width = og_ref.shape[1]
    for ref, items in (
        (up_ref, (None, 1)),
        (down_ref, (None, 7)),
        (up_two_ref, (4, None, 3, 2)),
        (down_two_ref, (None, 5, 6)),
        (kept_ref, (0,)),
    ):
        row = 0
        for shift in items:
            if shift is None:
                block = og_ref[...]
            else:
                start = pl.multiple_of(block_at(-shift, parts) * width, width)
                block = w_ref[:, pl.ds(start, width)]
            ref[row : row + block.shape[0], :] = block
            row += block.shape[0]


def chunk_kernel(parts, rim, starts, *refs):
    og_refs = refs[:parts]
    w_ref, v_ref, t_ref, o_ref, log_ref = refs[parts : parts + 5]
    out_ref, cg_ref, head_ref, tail_ref = refs[parts + 5 :]
    documents, tokens, channels = cg_ref.shape
    groups = out_ref.shape[0] // 12
    width = w_ref.shape[1] // parts

    def columns(shift):
        return pl.ds(pl.multiple_of(block_at(shift, parts) * width, width), width)

    total = None
    for shift in range(parts):
        block = og_refs[shift][starts[shift] : starts[shift] + documents * tokens, :]
        part = dot(block, w_ref[:, columns(shift)], NT)
        total = part if total is None else total + part
    for doc in range(documents):
        grad = total[doc * tokens : (doc + 1) * tokens]
        cg_ref[doc] = grad
        for ref, rows in ((head_ref, slice(0, rim)), (tail_ref, slice(tokens - rim, tokens))):
            high, low = halves(grad[rows])
            ref[doc, 0:rim, :] = v_ref[doc, rows, :]
            ref[doc, rim : 2 * rim, :] = high
            ref[doc, 2 * rim : 3 * rim, :] = low
        mix = pick(prod(t_ref[doc].T, grad))
        for seg in range(SEGS):
            row = doc * SEGS + seg
            rows = slice(seg * groups, (seg + 1) * groups)
            out_ref[pl.ds(row, groups, stride=12), :] = o_ref[doc, rows, :]
            out_ref[pl.ds(4 + row, groups, stride=12), :] = mix[rows]
    for row in range(4):
        out_ref[pl.ds(8 + row, groups, stride=12), :] = jnp.broadcast_to(
            log_ref[row : row + 1, :], (groups, channels)
        )


def landmark_units(scale, qm_ref, km_ref):
    count = qm_ref.shape[1]
    units = []
    for doc in range(qm_ref.shape[0]):
        scores = prod(stack(qm_ref[doc]), km_ref[doc], NT) * scale
        scores = jnp.exp(scores - jnp.max(scores, axis=1, keepdims=True))
        scores = scores / jnp.sum(scores, axis=1, keepdims=True)
        units += [scores[:count], scores[count:]]
    return units


def column_peak(unit):
    return jnp.max(jnp.sum(unit, axis=0, keepdims=True), axis=1, keepdims=True)


def newton(units, keep):
    every = range(len(units))
    count = units[0].shape[0]
    row = lax.broadcasted_iota(jnp.int32, (count, count), 0)
    identity = (row == lax.broadcasted_iota(jnp.int32, (count, count), 1)).astype(f32)
    approx = [unit.T / column_peak(unit) for unit in units]
    units = [halves(unit) for unit in units]
    for step in range(ITERS):
        spread = [halves(approx[i]) for i in every]
        product = [prod(units[i], spread[i]) for i in every]
        first = [7.0 * identity - product[i] for i in every]
        split = [halves(product[i]) for i in every]
        second = [15.0 * identity - prod(split[i], first[i]) for i in every]
        third = [13.0 * identity - prod(split[i], second[i]) for i in every]
        for i in every:
            keep(step, i, (approx[i], product[i], first[i], second[i], third[i]))
        if step < ITERS - 1 or not keep.last:
            approx = [0.25 * prod(spread[i], third[i]) for i in every]
    return approx


class Nothing:
    last = False

    def __call__(self, step, index, values):
        pass


class Kept:
    last = True

    def __init__(self, refs):
        self.refs = refs

    def __call__(self, step, index, values):
        for ref, value in zip(self.refs, values):
            ref[step, index] = value.T


def inverse_kernel(scale, qm_ref, km_ref, inv_ref):
    for index, unit in enumerate(newton(landmark_units(scale, qm_ref, km_ref), Nothing())):
        inv_ref[index] = unit


def turn_kernel(parts, starts, *refs):
    count, width = refs[parts].shape[1], refs[0].shape[1]
    for shift in range(parts):
        start = pl.multiple_of(block_at(shift, parts) * width, width)
        refs[parts][pl.ds(start, width), :] = refs[shift][starts[shift] : starts[shift] + count, :].T


def combine_kernel(got_ref, out_ref, log_ref):
    groups = got_ref.shape[0] // 12
    channels = got_ref.shape[1]
    me = lax.axis_index("seq")
    lane = lax.broadcasted_iota(jnp.int32, (groups, channels), 1)
    shares, logs = [], []
    for unit in range(4):
        log = got_ref[pl.ds(8 + unit, groups, stride=12), :]
        top = jnp.max(log, axis=0, keepdims=True)
        part = jnp.exp(log - top)
        total = jnp.sum(part, axis=0, keepdims=True)
        logs.append(top + jnp.log(total))
        shares.append(part / total)
    logs.append(jnp.zeros((4, channels), f32))
    log_ref[...] = jnp.concatenate(logs, axis=0)
    mixed, mix = [], []
    for doc in range(2):
        for seg in range(SEGS):
            row = doc * SEGS + seg
            weight = [
                jnp.sum(
                    jnp.where(lane == seg * groups + me, shares[doc * 2 + head], 0.0),
                    axis=1,
                    keepdims=True,
                )
                for head in range(2)
            ]
            weight = jnp.where(lane < channels // 2, weight[0], weight[1])
            mixed.append(
                jnp.sum(weight * got_ref[pl.ds(row, groups, stride=12), :], axis=0, keepdims=True)
            )
            mix.append(jnp.sum(got_ref[pl.ds(4 + row, groups, stride=12), :], axis=0, keepdims=True))
    block = jnp.concatenate(mixed + mix, axis=0)
    out_ref[...] = jnp.broadcast_to(block[None], out_ref.shape)


def conv_kernel(taps_ref, v_ref, cg_ref, above_ref, below_ref, conv_ref, back_ref, vp, cp):
    documents, tokens, channels = v_ref.shape
    taps = taps_ref.shape[0]
    rim = taps // 2
    for doc in range(documents):
        vp[doc, rim : rim + tokens, :] = v_ref[doc].astype(f32)
        cp[doc, rim : rim + tokens, :] = cg_ref[doc]
        for ref, start in ((above_ref, 0), (below_ref, rim + tokens)):
            rows = [ref[doc, i * rim : (i + 1) * rim, :].astype(f32) for i in range(3)]
            vp[doc, start : start + rim, :] = rows[0]
            cp[doc, start : start + rim, :] = rows[1] + rows[2]
    lane = lax.broadcasted_iota(jnp.int32, (1, channels), 1)
    for doc in range(documents):
        conv = jnp.zeros((tokens, channels), f32)
        back = jnp.zeros((tokens, channels), f32)
        for tap in range(taps):
            weight = jnp.where(lane < channels // 2, taps_ref[tap, 0], taps_ref[tap, 1])
            conv = conv + weight * vp[doc, tap : tap + tokens, :]
            start = 2 * rim - tap
            back = back + weight * cp[doc, start : start + tokens, :]
        conv_ref[doc] = conv
        back_ref[doc] = back


def context_kernel(
    got_ref, t_ref, inv_far, conv_far, ctx_ref, mixed_ref, mix_ref, lm_ref, inv_ref, conv_ref, sems
):
    fetches = [
        pltpu.make_async_copy(inv_far, inv_ref, sems.at[0]),
        pltpu.make_async_copy(conv_far, conv_ref, sems.at[1]),
    ]
    for fetch in fetches:
        fetch.start()
    for fetch in fetches:
        fetch.wait()
    documents, tokens, _ = conv_ref.shape
    groups = got_ref.shape[0] // 8
    for doc in range(documents):
        mixed = marks(got_ref, doc * SEGS, groups, 8)
        mixed_ref[doc] = mixed
        mix_ref[doc] = marks(got_ref, 4 + doc * SEGS, groups, 8)
        inverse = jnp.concatenate([inv_ref[doc * 2], inv_ref[doc * 2 + 1]], axis=0)
        landmark = own_blocks(prod(inverse, mixed))
        lm_ref[doc] = landmark
        ctx = (prod(t_ref[doc], landmark) + conv_ref[doc]).astype(bf16)
        ctx_ref[doc * tokens : (doc + 1) * tokens, :] = ctx


def token_back(scale, weights, grad, landmark):
    count = weights.shape[1] // 2
    back = weights * prod(grad, landmark, NT)
    return jnp.concatenate(
        [
            back[:, part] - weights[:, part] * jnp.sum(back[:, part], axis=1, keepdims=True)
            for part in (slice(0, count), slice(count, 2 * count))
        ],
        axis=1,
    ) * scale


def key_side(scale, doc, log_ref, s_ref, inv_ref, v_ref, mixed_ref, mix_ref):
    turned = jnp.concatenate([inv_ref[doc * 2].T, inv_ref[doc * 2 + 1].T], axis=0)
    mixed_grad = own_blocks(prod(turned, mix_ref[doc]))
    ones = jnp.ones((8, mixed_grad.shape[1]), bf16)
    mixed_dot = prod(ones, mixed_grad * stack(mixed_ref[doc]), NT)[0:1]
    mixed_grad = halves(mixed_grad)
    log = jnp.concatenate(
        [log_ref[doc * 2 : doc * 2 + 1, :], log_ref[doc * 2 + 1 : doc * 2 + 2, :]], axis=1
    )
    key_weights = jnp.exp(s_ref[doc] - log)
    key_back = key_weights * (prod(v_ref[doc], mixed_grad, NT) - mixed_dot) * scale
    return key_weights, key_back, mixed_grad


def main_kernel(
    scale, log_ref, t_ref, s_ref, cg_ref, inv_ref, q_ref, k_ref, v_ref, ogt_ref, ctx_ref,
    mixed_ref, mix_ref, lm_ref, out_far, out_ref, held, sems,
):
    documents, tokens, channels = q_ref.shape
    groups = out_ref.shape[0]
    terms = dot(ogt_ref[...], ctx_ref[...]).astype(bf16)
    out_ref[:, 16:, :] = terms.reshape(groups, terms.shape[0] // groups, channels)
    rest = pltpu.make_async_copy(out_ref.at[:, 16:, :], out_far.at[:, 16:, :], sems.at[0])
    rest.start()
    for doc in range(documents):
        back = token_back(scale, t_ref[doc], cg_ref[doc], lm_ref[doc])
        key_terms = pick(prod(back.T, q_ref[doc]))
        _, key_back, _ = key_side(scale, doc, log_ref, s_ref, inv_ref, v_ref, mixed_ref, mix_ref)
        query_terms = pick(prod(key_back.T, k_ref[doc]))
        for base, terms in ((0, query_terms), (4, key_terms)):
            high = terms.astype(bf16).astype(f32)
            low = terms - high
            for seg in range(SEGS):
                row = base + doc * SEGS + seg
                rows = slice(seg * groups, (seg + 1) * groups)
                held[pl.ds(row, groups, stride=16), :] = high[rows]
                held[pl.ds(8 + row, groups, stride=16), :] = low[rows]
    out_ref[:, 0:16, :] = held[...].astype(bf16).reshape(groups, 16, channels)
    first = pltpu.make_async_copy(out_ref.at[:, 0:16, :], out_far.at[:, 0:16, :], sems.at[1])
    first.start()
    rest.wait()
    first.wait()


def direct_kernel(
    scale, log_ref, t_ref, s_ref, cg_ref, qm_ref, km_ref, inv_ref, v_ref, back_ref, mixed_ref,
    mix_ref, qd_ref, kd_ref, vg_ref,
):
    for doc in range(v_ref.shape[0]):
        inverse = jnp.concatenate([inv_ref[doc * 2], inv_ref[doc * 2 + 1]], axis=0)
        landmark = own_blocks(prod(inverse, mixed_ref[doc]))
        back = token_back(scale, t_ref[doc], cg_ref[doc], landmark)
        qd_ref[doc] = prod(back, stack(km_ref[doc]))
        key_weights, key_back, mixed_grad = key_side(
            scale, doc, log_ref, s_ref, inv_ref, v_ref, mixed_ref, mix_ref
        )
        kd_ref[doc] = prod(key_back, stack(qm_ref[doc]))
        vg_ref[doc] = (prod(key_weights, mixed_grad) + back_ref[doc]).astype(bf16)


def newton_back_kernel(scale, qm_ref, km_ref, mixed_ref, mix_ref, out_ref, held, *kept):
    documents, count, channels = qm_ref.shape
    me = lax.axis_index("seq")
    groups = count // SEGS
    every = range(documents * 2)
    units = landmark_units(scale, qm_ref, km_ref)
    newton(units, Kept(kept))
    approx_t, product_t, first_t, second_t, third_t = kept
    down = []
    for doc in range(documents):
        full = prod(stack(mix_ref[doc]), mixed_ref[doc], NT)
        down += [full[:count], full[count:]]
    unit_t = [halves(units[i].T) for i in every]
    grads = [None for i in every]
    for step in reversed(range(ITERS)):
        down = [halves(0.25 * down[i]) for i in every]
        turned = [halves(approx_t[step, i]) for i in every]
        product = [halves(product_t[step, i]) for i in every]
        third = [prod(turned[i], down[i]) for i in every]
        third = [halves(third[i]) for i in every]
        carry = [prod(down[i], third_t[step, i]) for i in every]
        second = [-prod(product[i], third[i]) for i in every]
        second = [halves(second[i]) for i in every]
        first = [-prod(product[i], second[i]) for i in every]
        flow = [
            -first[i] - prod(third[i], second_t[step, i]) - prod(second[i], first_t[step, i])
            for i in every
        ]
        flow = [halves(flow[i]) for i in every]
        more = [prod(flow[i], turned[i]) for i in every]
        grads = [more[i] if grads[i] is None else grads[i] + more[i] for i in every]
        down = [carry[i] + prod(unit_t[i], flow[i]) for i in every]
    for doc in range(documents):
        back, turned = [], []
        for head in range(2):
            i = doc * 2 + head
            unit = units[i]
            grad = grads[i] + down[i].T / column_peak(unit)
            part = unit * grad
            part = (part - unit * jnp.sum(part, axis=1, keepdims=True)) * scale
            back.append(part)
            turned.append(part.T)
        held[doc] = pick(prod(jnp.concatenate(back, axis=0), km_ref[doc]))
        held[documents + doc] = pick(prod(jnp.concatenate(turned, axis=0), qm_ref[doc]))
    for kind in range(2 * documents):
        for seg in range(SEGS):
            out_row = kind * SEGS + seg
            out_ref[out_row : out_row + 1, :] = held[kind, pl.ds(seg * groups + me, 1), :]


def finish_kernel(got_ref, own_ref, qd_ref, kd_ref, qg_ref, kg_ref, wg_ref):
    documents, tokens, _ = qd_ref.shape
    segment = tokens // SEGS
    total = jnp.sum(got_ref[:, 0:16, :].astype(f32), axis=0)
    total = (total[0:8] + total[8:16] + own_ref[...]) * (1.0 / segment)
    for base, source, target in ((0, qd_ref, qg_ref), (4, kd_ref, kg_ref)):
        for doc in range(documents):
            for seg in range(SEGS):
                row = base + doc * SEGS + seg
                rows = slice(seg * segment, (seg + 1) * segment)
                target[doc, rows, :] = (source[doc, rows, :] + total[row : row + 1]).astype(bf16)
    wg_ref[...] = jnp.sum(got_ref[:, 16:, :].astype(f32), axis=0)


def output_kernel(blocks, weights, *refs):
    total = None
    tokens = refs[-1].shape[0]
    channels = refs[0].shape[1]
    for (index, block), (source, row) in zip(blocks, weights):
        weight = refs[source][row : row + channels, :]
        part = dot(refs[index][block * tokens : (block + 1) * tokens, :], weight)
        total = part if total is None else total + part
    refs[-1][...] = total.astype(bf16)


def call(kernel, outs, *operands, scratch=(), smem=(), far=(), far_out=False, flops=1e8, size=2e6):
    vmem = pl.BlockSpec(memory_space=pltpu.VMEM)
    scalar = pl.BlockSpec(memory_space=pltpu.SMEM)
    anywhere = pl.BlockSpec(memory_space=pl.ANY)
    return pl.pallas_call(
        kernel,
        out_shape=[jax.ShapeDtypeStruct(shape, kind) for shape, kind in outs],
        in_specs=[
            scalar if i in smem else anywhere if i in far else vmem for i in range(len(operands))
        ],
        out_specs=[anywhere if far_out else vmem for _ in outs],
        scratch_shapes=list(scratch),
        compiler_params=pltpu.CompilerParams(vmem_limit_bytes=16 * 1024 * 1024),
        cost_estimate=pl.CostEstimate(
            flops=int(flops), bytes_accessed=int(size), transcendentals=0
        ),
    )(*operands)


def exchange(blocks, axis):
    return lax.all_to_all(blocks, axis, 0, 0, tiled=True)


def shift_by(block, shift, parts):
    pairs = []
    for i in range(lax.axis_size("seq")):
        step = shift if i % 2 == 0 else parts - shift
        pairs += [(i * parts + j, i * parts + (j + step) % parts) for j in range(parts)]
    return lax.ppermute(block, ("seq", "head"), pairs)


def shards(queries, key_vectors, value_vectors, conv_taps, out_weight, out_grad):
    documents, tokens, channels = queries.shape
    heads = conv_taps.shape[1]
    groups = lax.axis_size("seq")
    parts = lax.axis_size("head")
    count = SEGS * groups
    scale = (channels // heads) ** (-0.5)
    rim = conv_taps.shape[0] // 2
    model_width = out_weight.shape[1]
    own_width = model_width // parts
    column_rows = model_width // groups
    rows_shape = (documents, tokens, channels)
    marks_shape = (documents, count, channels)
    pair_shape = (documents, tokens, 2 * count)
    units = 2 * documents
    saved = (ITERS, units, count, count)

    (sent,) = call(means_kernel, [((groups, 8, channels), f32)], queries, key_vectors)
    own_grad, sent = lax.optimization_barrier((out_grad, sent))
    got = exchange(sent, "seq").reshape(groups * 8, channels)
    own_grad = own_grad.reshape(documents * tokens, own_width)
    rows = documents * tokens
    up, down, up_two, down_two, kept = call(
        functools.partial(pack_kernel, parts),
        [((rows + pieces * channels, own_width), bf16) for pieces in (1, 1, 3, 2)]
        + [((channels, own_width), bf16)],
        own_grad, out_weight,
    )
    up_two, down_two = shift_by(up_two, 2, parts), shift_by(down_two, parts - 2, parts)
    up, down = shift_by(up, 1, parts), shift_by(down, parts - 1, parts)
    up_three = shift_by(up_two[channels : rows + 2 * channels], 1, parts)
    down_three = shift_by(down_two[: rows + channels], parts - 1, parts)
    across = shift_by(up_two[: rows + channels], 2, parts)
    og_parts = [own_grad, up, up_two, up_three, across, down_three, down_two, down]
    og_starts = (0, 0, channels, 0, channels, 0, 0, 0)
    w_starts = (0, rows, rows + 2 * channels, rows, 0, rows, rows + channels, rows)

    weights, scores, local_mixed, local_log, qm, km = call(
        functools.partial(stats_kernel, scale),
        [
            (pair_shape, f32),
            (pair_shape, f32),
            (marks_shape, f32),
            ((8, count), f32),
            (marks_shape, f32),
            (marks_shape, f32),
        ],
        got, queries, key_vectors, value_vectors,
    )
    sent, context_grad, first_rows, last_rows = call(
        functools.partial(chunk_kernel, parts, rim, og_starts),
        [((groups * 12, channels), f32), (rows_shape, f32)]
        + [((documents, 3 * rim, channels), bf16)] * 2,
        *og_parts, out_weight, value_vectors, weights, local_mixed, local_log,
    )
    sent, qm, km = lax.optimization_barrier((sent, qm, km))
    got = exchange(sent.reshape(groups, 3, 4, channels), "seq").reshape(groups * 12, channels)
    ends = groups - 1
    above = lax.ppermute(last_rows, "seq", [(i, i + 1) for i in range(ends)])
    below = lax.ppermute(first_rows, "seq", [(i + 1, i) for i in range(ends)])
    (inverse,) = call(
        functools.partial(inverse_kernel, scale), [((units, count, count), f32)], qm, km, flops=2e9
    )
    got, above, below, inverse = lax.optimization_barrier((got, above, below, inverse))
    sent, logs = call(
        combine_kernel, [((groups, 8, channels), f32), ((8, count), f32)], got
    )
    sent, og_parts = lax.optimization_barrier((sent, og_parts))
    (og_turned,) = call(
        functools.partial(turn_kernel, parts, og_starts), [((model_width, documents * tokens), bf16)], *og_parts
    )
    got = exchange(sent, "seq").reshape(groups * 8, channels)
    conv, back = call(
        conv_kernel,
        [(rows_shape, f32), (rows_shape, f32)],
        conv_taps, value_vectors, context_grad, above, below,
        scratch=[pltpu.VMEM((documents, tokens + 2 * rim, channels), f32)] * 2,
        smem=(0,),
        flops=1e9,
    )
    got, conv, back, og_turned = lax.optimization_barrier((got, conv, back, og_turned))
    weight_parts = [kept] + og_parts[1:]
    context_b, mixed, mix, landmark_mix = call(
        context_kernel,
        [
            ((documents * tokens, channels), bf16),
            (marks_shape, f32),
            (marks_shape, f32),
            ((documents, 2 * count, channels), f32),
        ],
        got, weights, inverse, conv,
        scratch=[
            pltpu.VMEM((units, count, count), f32),
            pltpu.VMEM(rows_shape, f32),
            pltpu.SemaphoreType.DMA((2,)),
        ],
        far=(2, 3),
    )
    near = [shift_by(context_b, 1, parts), shift_by(context_b, parts - 1, parts)]
    sent_shape = (groups, 16 + column_rows, channels)
    (sent,) = call(
        functools.partial(main_kernel, scale),
        [(sent_shape, bf16)],
        logs, weights, scores, context_grad, inverse, queries, key_vectors, value_vectors,
        og_turned, context_b, mixed, mix, landmark_mix,
        scratch=[
            pltpu.VMEM(sent_shape, bf16),
            pltpu.VMEM((groups * 16, channels), f32),
            pltpu.SemaphoreType.DMA((2,)),
        ],
        far_out=True,
        flops=1e9,
    )
    sent, near, mix = lax.optimization_barrier((sent, near, mix))
    got = exchange(sent, "seq")
    query_direct, key_direct, value_grad = call(
        functools.partial(direct_kernel, scale),
        [(rows_shape, f32), (rows_shape, f32), (rows_shape, bf16)],
        logs, weights, scores, context_grad, qm, km, inverse, value_vectors, back, mixed, mix,
        flops=1e9,
    )
    far = [
        shift_by(jnp.concatenate([near[0], context_b, near[1]], axis=0), 3, parts),
        shift_by(jnp.concatenate([near[0], context_b], axis=0), parts - 3, parts),
    ]
    (own,) = call(
        functools.partial(newton_back_kernel, scale),
        [((8, channels), f32)],
        qm, km, mixed, mix,
        scratch=[pltpu.VMEM((2 * documents, count, channels), f32)] + [pltpu.VMEM(saved, f32)] * 5,
        flops=5e9,
    )
    blocks = ((0, 0), (1, 0), (3, 2), (3, 1), (3, 0), (4, 1), (4, 0), (2, 0))
    slots = tuple((5 + shift, start) for shift, start in enumerate(w_starts))
    (layer_output,) = call(
        functools.partial(output_kernel, blocks, slots),
        [((documents * tokens, own_width), bf16)],
        context_b, *near, *far, *weight_parts,
    )
    query_grad, key_grad, weight_grad = call(
        finish_kernel,
        [(rows_shape, bf16), (rows_shape, bf16), ((column_rows, channels), f32)],
        got, own, query_direct, key_direct,
    )
    return (
        layer_output.reshape(documents, tokens, own_width),
        query_grad,
        key_grad,
        value_grad,
        weight_grad.T,
    )


def solution(mesh):
    in_specs = (
        P(None, "seq", "head"),
        P(None, "seq", "head"),
        P(None, "seq", "head"),
        P(None, "head"),
        P("head", None),
        P(None, "seq", "head"),
    )
    out_specs = (
        P(None, "seq", "head"),
        P(None, "seq", "head"),
        P(None, "seq", "head"),
        P(None, "seq", "head"),
        P("head", "seq"),
    )
    return jax.shard_map(shards, mesh=mesh, in_specs=in_specs, out_specs=out_specs, check_vma=False)
```

```python
import functools

import jax
import jax.numpy as jnp
from jax import lax
from jax.experimental import pallas as pl
from jax.experimental.pallas import tpu as pltpu
from jax.sharding import PartitionSpec as P

ITERS = 2
SEGS = 2
f32 = jnp.float32
bf16 = jnp.bfloat16
NN = (((1,), (0,)), ((), ()))
NT = (((1,), (1,)), ((), ()))


def dot(left, right, dims=NN):
    return lax.dot_general(left, right, dims, preferred_element_type=f32)


def halves(value):
    if value.dtype == bf16:
        return (value,)
    high = value.astype(bf16)
    return high, (value - high.astype(f32)).astype(bf16)


def prod(left, right, dims=NN):
    left = left if isinstance(left, tuple) else halves(left)
    right = right if isinstance(right, tuple) else halves(right)
    total = dot(left[0], right[0], dims)
    if len(right) > 1:
        total = total + dot(left[0], right[1], dims)
    if len(left) > 1:
        total = total + dot(left[1], right[0], dims)
    return total


def block_at(shift, parts):
    core = lax.rem(lax.axis_index("seq"), 2)
    step = jnp.where(core == 0, parts - shift, parts + shift)
    return lax.rem(lax.axis_index("head") + step, parts)


def first_head(shape):
    return lax.broadcasted_iota(jnp.int32, shape, 1) < shape[1] // 2


def stack(rows):
    mask = first_head(rows.shape)
    zero = jnp.zeros_like(rows)
    return jnp.concatenate([jnp.where(mask, rows, zero), jnp.where(mask, zero, rows)], axis=0)


def own_blocks(full):
    count = full.shape[0] // 2
    mask = first_head((count, full.shape[1]))
    zero = jnp.zeros((count, full.shape[1]), full.dtype)
    return jnp.concatenate(
        [jnp.where(mask, full[:count], zero), jnp.where(mask, zero, full[count:])], axis=0
    )


def pick(full):
    count = full.shape[0] // 2
    return jnp.where(first_head((count, full.shape[1])), full[:count], full[count:])


def marks(ref, row, groups, stride):
    return jnp.concatenate(
        [ref[pl.ds(row + seg, groups, stride=stride), :] for seg in range(SEGS)], axis=0
    )


def means_kernel(q_ref, k_ref, out_ref):
    documents, tokens, _ = q_ref.shape
    segment = tokens // SEGS
    rows = []
    for ref in (q_ref, k_ref):
        for doc in range(documents):
            for seg in range(SEGS):
                part = ref[doc, seg * segment : (seg + 1) * segment, :].astype(f32)
                rows.append(jnp.sum(part, axis=0, keepdims=True) * (1.0 / segment))
    block = jnp.concatenate(rows, axis=0)
    out_ref[...] = jnp.broadcast_to(block[None], out_ref.shape)


def stats_kernel(scale, got_ref, q_ref, k_ref, v_ref, t_ref, s_ref, o_ref, log_ref, qm_ref, km_ref):
    documents = q_ref.shape[0]
    groups = got_ref.shape[0] // 8
    count = SEGS * groups
    logs = []
    for doc in range(documents):
        qm = marks(got_ref, doc * SEGS, groups, 8)
        km = marks(got_ref, 4 + doc * SEGS, groups, 8)
        qm_ref[doc] = qm
        km_ref[doc] = km
        scores = prod(q_ref[doc], stack(km), NT) * scale
        for head in range(2):
            part = scores[:, head * count : (head + 1) * count]
            part = jnp.exp(part - jnp.max(part, axis=1, keepdims=True))
            t_ref[doc, :, head * count : (head + 1) * count] = part / jnp.sum(
                part, axis=1, keepdims=True
            )
        scores = prod(k_ref[doc], stack(qm), NT) * scale
        s_ref[doc] = scores
        peak = jnp.max(scores, axis=0, keepdims=True)
        part = jnp.exp(scores - peak)
        total = jnp.sum(part, axis=0, keepdims=True)
        o_ref[doc] = pick(prod((part / total).T, v_ref[doc]))
        log = peak + jnp.log(total)
        logs += [log[:, :count], log[:, count:]]
    logs.append(jnp.zeros((8 - len(logs), count), f32))
    log_ref[...] = jnp.concatenate(logs, axis=0)


def pack_kernel(parts, og_ref, w_ref, up_ref, down_ref, up_two_ref, down_two_ref, kept_ref):
    width = og_ref.shape[1]
    for ref, items in (
        (up_ref, (None, 1)),
        (down_ref, (None, 7)),
        (up_two_ref, (4, None, 3, 2)),
        (down_two_ref, (None, 5, 6)),
        (kept_ref, (0,)),
    ):
        row = 0
        for shift in items:
            if shift is None:
                block = og_ref[...]
            else:
                start = pl.multiple_of(block_at(-shift, parts) * width, width)
                block = w_ref[:, pl.ds(start, width)]
            ref[row : row + block.shape[0], :] = block
            row += block.shape[0]


def chunk_kernel(parts, rim, starts, *refs):
    og_refs = refs[:parts]
    w_ref, v_ref, t_ref, o_ref, log_ref = refs[parts : parts + 5]
    out_ref, cg_ref, head_ref, tail_ref = refs[parts + 5 :]
    documents, tokens, channels = cg_ref.shape
    groups = out_ref.shape[0] // 12
    width = w_ref.shape[1] // parts

    def columns(shift):
        return pl.ds(pl.multiple_of(block_at(shift, parts) * width, width), width)

    total = None
    for shift in range(parts):
        block = og_refs[shift][starts[shift] : starts[shift] + documents * tokens, :]
        part = dot(block, w_ref[:, columns(shift)], NT)
        total = part if total is None else total + part
    for doc in range(documents):
        grad = total[doc * tokens : (doc + 1) * tokens]
        cg_ref[doc] = grad
        for ref, rows in ((head_ref, slice(0, rim)), (tail_ref, slice(tokens - rim, tokens))):
            high, low = halves(grad[rows])
            ref[doc, 0:rim, :] = v_ref[doc, rows, :]
            ref[doc, rim : 2 * rim, :] = high
            ref[doc, 2 * rim : 3 * rim, :] = low
        mix = pick(prod(t_ref[doc].T, grad))
        for seg in range(SEGS):
            row = doc * SEGS + seg
            rows = slice(seg * groups, (seg + 1) * groups)
            out_ref[pl.ds(row, groups, stride=12), :] = o_ref[doc, rows, :]
            out_ref[pl.ds(4 + row, groups, stride=12), :] = mix[rows]
    for row in range(4):
        out_ref[pl.ds(8 + row, groups, stride=12), :] = jnp.broadcast_to(
            log_ref[row : row + 1, :], (groups, channels)
        )


def landmark_units(scale, qm_ref, km_ref):
    count = qm_ref.shape[1]
    units = []
    for doc in range(qm_ref.shape[0]):
        scores = prod(stack(qm_ref[doc]), km_ref[doc], NT) * scale
        scores = jnp.exp(scores - jnp.max(scores, axis=1, keepdims=True))
        scores = scores / jnp.sum(scores, axis=1, keepdims=True)
        units += [scores[:count], scores[count:]]
    return units


def column_peak(unit):
    return jnp.max(jnp.sum(unit, axis=0, keepdims=True), axis=1, keepdims=True)


def newton(units, keep):
    every = range(len(units))
    count = units[0].shape[0]
    row = lax.broadcasted_iota(jnp.int32, (count, count), 0)
    identity = (row == lax.broadcasted_iota(jnp.int32, (count, count), 1)).astype(f32)
    approx = [unit.T / column_peak(unit) for unit in units]
    units = [halves(unit) for unit in units]
    for step in range(ITERS):
        spread = [halves(approx[i]) for i in every]
        product = [prod(units[i], spread[i]) for i in every]
        first = [7.0 * identity - product[i] for i in every]
        split = [halves(product[i]) for i in every]
        second = [15.0 * identity - prod(split[i], first[i]) for i in every]
        third = [13.0 * identity - prod(split[i], second[i]) for i in every]
        for i in every:
            keep(step, i, (approx[i], product[i], first[i], second[i], third[i]))
        if step < ITERS - 1 or not keep.last:
            approx = [0.25 * prod(spread[i], third[i]) for i in every]
    return approx


class Nothing:
    last = False

    def __call__(self, step, index, values):
        pass


class Kept:
    last = True

    def __init__(self, refs):
        self.refs = refs

    def __call__(self, step, index, values):
        for ref, value in zip(self.refs, values):
            ref[step, index] = value.T


def inverse_kernel(scale, qm_ref, km_ref, inv_ref):
    for index, unit in enumerate(newton(landmark_units(scale, qm_ref, km_ref), Nothing())):
        inv_ref[index] = unit


def turn_kernel(parts, starts, *refs):
    count, width = refs[parts].shape[1], refs[0].shape[1]
    for shift in range(parts):
        start = pl.multiple_of(block_at(shift, parts) * width, width)
        refs[parts][pl.ds(start, width), :] = refs[shift][starts[shift] : starts[shift] + count, :].T


def combine_kernel(got_ref, out_ref, log_ref):
    groups = got_ref.shape[0] // 12
    channels = got_ref.shape[1]
    me = lax.axis_index("seq")
    lane = lax.broadcasted_iota(jnp.int32, (groups, channels), 1)
    shares, logs = [], []
    for unit in range(4):
        log = got_ref[pl.ds(8 + unit, groups, stride=12), :]
        top = jnp.max(log, axis=0, keepdims=True)
        part = jnp.exp(log - top)
        total = jnp.sum(part, axis=0, keepdims=True)
        logs.append(top + jnp.log(total))
        shares.append(part / total)
    logs.append(jnp.zeros((4, channels), f32))
    log_ref[...] = jnp.concatenate(logs, axis=0)
    mixed, mix = [], []
    for doc in range(2):
        for seg in range(SEGS):
            row = doc * SEGS + seg
            weight = [
                jnp.sum(
                    jnp.where(lane == seg * groups + me, shares[doc * 2 + head], 0.0),
                    axis=1,
                    keepdims=True,
                )
                for head in range(2)
            ]
            weight = jnp.where(lane < channels // 2, weight[0], weight[1])
            mixed.append(
                jnp.sum(weight * got_ref[pl.ds(row, groups, stride=12), :], axis=0, keepdims=True)
            )
            mix.append(jnp.sum(got_ref[pl.ds(4 + row, groups, stride=12), :], axis=0, keepdims=True))
    block = jnp.concatenate(mixed + mix, axis=0)
    out_ref[...] = jnp.broadcast_to(block[None], out_ref.shape)


def conv_kernel(taps_ref, v_ref, cg_ref, above_ref, below_ref, conv_ref, back_ref, vp, cp):
    documents, tokens, channels = v_ref.shape
    taps = taps_ref.shape[0]
    rim = taps // 2
    for doc in range(documents):
        vp[doc, rim : rim + tokens, :] = v_ref[doc].astype(f32)
        cp[doc, rim : rim + tokens, :] = cg_ref[doc]
        for ref, start in ((above_ref, 0), (below_ref, rim + tokens)):
            rows = [ref[doc, i * rim : (i + 1) * rim, :].astype(f32) for i in range(3)]
            vp[doc, start : start + rim, :] = rows[0]
            cp[doc, start : start + rim, :] = rows[1] + rows[2]
    lane = lax.broadcasted_iota(jnp.int32, (1, channels), 1)
    for doc in range(documents):
        conv = jnp.zeros((tokens, channels), f32)
        back = jnp.zeros((tokens, channels), f32)
        for tap in range(taps):
            weight = jnp.where(lane < channels // 2, taps_ref[tap, 0], taps_ref[tap, 1])
            conv = conv + weight * vp[doc, tap : tap + tokens, :]
            start = 2 * rim - tap
            back = back + weight * cp[doc, start : start + tokens, :]
        conv_ref[doc] = conv
        back_ref[doc] = back


def context_kernel(
    got_ref, t_ref, inv_far, conv_far, ctx_ref, mixed_ref, mix_ref, lm_ref, inv_ref, conv_ref, sems
):
    fetches = [
        pltpu.make_async_copy(inv_far, inv_ref, sems.at[0]),
        pltpu.make_async_copy(conv_far, conv_ref, sems.at[1]),
    ]
    for fetch in fetches:
        fetch.start()
    for fetch in fetches:
        fetch.wait()
    documents, tokens, _ = conv_ref.shape
    groups = got_ref.shape[0] // 8
    for doc in range(documents):
        mixed = marks(got_ref, doc * SEGS, groups, 8)
        mixed_ref[doc] = mixed
        mix_ref[doc] = marks(got_ref, 4 + doc * SEGS, groups, 8)
        inverse = jnp.concatenate([inv_ref[doc * 2], inv_ref[doc * 2 + 1]], axis=0)
        landmark = own_blocks(prod(inverse, mixed))
        lm_ref[doc] = landmark
        ctx = (prod(t_ref[doc], landmark) + conv_ref[doc]).astype(bf16)
        ctx_ref[doc * tokens : (doc + 1) * tokens, :] = ctx


def token_back(scale, weights, grad, landmark):
    count = weights.shape[1] // 2
    back = weights * prod(grad, landmark, NT)
    return jnp.concatenate(
        [
            back[:, part] - weights[:, part] * jnp.sum(back[:, part], axis=1, keepdims=True)
            for part in (slice(0, count), slice(count, 2 * count))
        ],
        axis=1,
    ) * scale


def key_side(scale, doc, log_ref, s_ref, inv_ref, v_ref, mixed_ref, mix_ref):
    turned = jnp.concatenate([inv_ref[doc * 2].T, inv_ref[doc * 2 + 1].T], axis=0)
    mixed_grad = own_blocks(prod(turned, mix_ref[doc]))
    ones = jnp.ones((8, mixed_grad.shape[1]), bf16)
    mixed_dot = prod(ones, mixed_grad * stack(mixed_ref[doc]), NT)[0:1]
    mixed_grad = halves(mixed_grad)
    log = jnp.concatenate(
        [log_ref[doc * 2 : doc * 2 + 1, :], log_ref[doc * 2 + 1 : doc * 2 + 2, :]], axis=1
    )
    key_weights = jnp.exp(s_ref[doc] - log)
    key_back = key_weights * (prod(v_ref[doc], mixed_grad, NT) - mixed_dot) * scale
    return key_weights, key_back, mixed_grad


def main_kernel(
    scale, log_ref, t_ref, s_ref, cg_ref, inv_ref, q_ref, k_ref, v_ref, ogt_ref, ctx_ref,
    mixed_ref, mix_ref, lm_ref, out_far, out_ref, held, sems,
):
    documents, tokens, channels = q_ref.shape
    groups = out_ref.shape[0]
    terms = dot(ogt_ref[...], ctx_ref[...]).astype(bf16)
    out_ref[:, 16:, :] = terms.reshape(groups, terms.shape[0] // groups, channels)
    rest = pltpu.make_async_copy(out_ref.at[:, 16:, :], out_far.at[:, 16:, :], sems.at[0])
    rest.start()
    for doc in range(documents):
        back = token_back(scale, t_ref[doc], cg_ref[doc], lm_ref[doc])
        key_terms = pick(prod(back.T, q_ref[doc]))
        _, key_back, _ = key_side(scale, doc, log_ref, s_ref, inv_ref, v_ref, mixed_ref, mix_ref)
        query_terms = pick(prod(key_back.T, k_ref[doc]))
        for base, terms in ((0, query_terms), (4, key_terms)):
            high = terms.astype(bf16).astype(f32)
            low = terms - high
            for seg in range(SEGS):
                row = base + doc * SEGS + seg
                rows = slice(seg * groups, (seg + 1) * groups)
                held[pl.ds(row, groups, stride=16), :] = high[rows]
                held[pl.ds(8 + row, groups, stride=16), :] = low[rows]
    out_ref[:, 0:16, :] = held[...].astype(bf16).reshape(groups, 16, channels)
    first = pltpu.make_async_copy(out_ref.at[:, 0:16, :], out_far.at[:, 0:16, :], sems.at[1])
    first.start()
    rest.wait()
    first.wait()


def direct_kernel(
    scale, log_ref, t_ref, s_ref, cg_ref, qm_ref, km_ref, inv_ref, v_ref, back_ref, mixed_ref,
    mix_ref, qd_ref, kd_ref, vg_ref,
):
    for doc in range(v_ref.shape[0]):
        inverse = jnp.concatenate([inv_ref[doc * 2], inv_ref[doc * 2 + 1]], axis=0)
        landmark = own_blocks(prod(inverse, mixed_ref[doc]))
        back = token_back(scale, t_ref[doc], cg_ref[doc], landmark)
        qd_ref[doc] = prod(back, stack(km_ref[doc]))
        key_weights, key_back, mixed_grad = key_side(
            scale, doc, log_ref, s_ref, inv_ref, v_ref, mixed_ref, mix_ref
        )
        kd_ref[doc] = prod(key_back, stack(qm_ref[doc]))
        vg_ref[doc] = (prod(key_weights, mixed_grad) + back_ref[doc]).astype(bf16)


def newton_back_kernel(scale, qm_ref, km_ref, mixed_ref, mix_ref, out_ref, held, *kept):
    documents, count, channels = qm_ref.shape
    me = lax.axis_index("seq")
    groups = count // SEGS
    every = range(documents * 2)
    units = landmark_units(scale, qm_ref, km_ref)
    newton(units, Kept(kept))
    approx_t, product_t, first_t, second_t, third_t = kept
    down = []
    for doc in range(documents):
        full = prod(stack(mix_ref[doc]), mixed_ref[doc], NT)
        down += [full[:count], full[count:]]
    unit_t = [halves(units[i].T) for i in every]
    grads = [None for i in every]
    for step in reversed(range(ITERS)):
        down = [halves(0.25 * down[i]) for i in every]
        turned = [halves(approx_t[step, i]) for i in every]
        product = [halves(product_t[step, i]) for i in every]
        third = [prod(turned[i], down[i]) for i in every]
        third = [halves(third[i]) for i in every]
        carry = [prod(down[i], third_t[step, i]) for i in every]
        second = [-prod(product[i], third[i]) for i in every]
        second = [halves(second[i]) for i in every]
        first = [-prod(product[i], second[i]) for i in every]
        flow = [
            -first[i] - prod(third[i], second_t[step, i]) - prod(second[i], first_t[step, i])
            for i in every
        ]
        flow = [halves(flow[i]) for i in every]
        more = [prod(flow[i], turned[i]) for i in every]
        grads = [more[i] if grads[i] is None else grads[i] + more[i] for i in every]
        down = [carry[i] + prod(unit_t[i], flow[i]) for i in every]
    for doc in range(documents):
        back, turned = [], []
        for head in range(2):
            i = doc * 2 + head
            unit = units[i]
            grad = grads[i] + down[i].T / column_peak(unit)
            part = unit * grad
            part = (part - unit * jnp.sum(part, axis=1, keepdims=True)) * scale
            back.append(part)
            turned.append(part.T)
        held[doc] = pick(prod(jnp.concatenate(back, axis=0), km_ref[doc]))
        held[documents + doc] = pick(prod(jnp.concatenate(turned, axis=0), qm_ref[doc]))
    for kind in range(2 * documents):
        for seg in range(SEGS):
            out_row = kind * SEGS + seg
            out_ref[out_row : out_row + 1, :] = held[kind, pl.ds(seg * groups + me, 1), :]


def finish_kernel(got_ref, own_ref, qd_ref, kd_ref, qg_ref, kg_ref, wg_ref):
    documents, tokens, _ = qd_ref.shape
    segment = tokens // SEGS
    total = jnp.sum(got_ref[:, 0:16, :].astype(f32), axis=0)
    total = (total[0:8] + total[8:16] + own_ref[...]) * (1.0 / segment)
    for base, source, target in ((0, qd_ref, qg_ref), (4, kd_ref, kg_ref)):
        for doc in range(documents):
            for seg in range(SEGS):
                row = base + doc * SEGS + seg
                rows = slice(seg * segment, (seg + 1) * segment)
                target[doc, rows, :] = (source[doc, rows, :] + total[row : row + 1]).astype(bf16)
    wg_ref[...] = jnp.sum(got_ref[:, 16:, :].astype(f32), axis=0)


def output_kernel(blocks, weights, *refs):
    total = None
    tokens = refs[-1].shape[0]
    channels = refs[0].shape[1]
    for (index, block), (source, row) in zip(blocks, weights):
        weight = refs[source][row : row + channels, :]
        part = dot(refs[index][block * tokens : (block + 1) * tokens, :], weight)
        total = part if total is None else total + part
    refs[-1][...] = total.astype(bf16)


def call(kernel, outs, *operands, scratch=(), smem=(), far=(), far_out=False, grant=16, flops=1e8, size=2e6):
    vmem = pl.BlockSpec(memory_space=pltpu.VMEM)
    scalar = pl.BlockSpec(memory_space=pltpu.SMEM)
    anywhere = pl.BlockSpec(memory_space=pl.ANY)
    return pl.pallas_call(
        kernel,
        out_shape=[jax.ShapeDtypeStruct(shape, kind) for shape, kind in outs],
        in_specs=[
            scalar if i in smem else anywhere if i in far else vmem for i in range(len(operands))
        ],
        out_specs=[anywhere if far_out else vmem for _ in outs],
        scratch_shapes=list(scratch),
        compiler_params=pltpu.CompilerParams(vmem_limit_bytes=grant * 1024 * 1024),
        cost_estimate=pl.CostEstimate(
            flops=int(flops), bytes_accessed=int(size), transcendentals=0
        ),
    )(*operands)


def exchange(blocks, axis):
    return lax.all_to_all(blocks, axis, 0, 0, tiled=True)


def shift_by(block, shift, parts):
    pairs = []
    for i in range(lax.axis_size("seq")):
        step = shift if i % 2 == 0 else parts - shift
        pairs += [(i * parts + j, i * parts + (j + step) % parts) for j in range(parts)]
    return lax.ppermute(block, ("seq", "head"), pairs)


def shards(queries, key_vectors, value_vectors, conv_taps, out_weight, out_grad):
    documents, tokens, channels = queries.shape
    heads = conv_taps.shape[1]
    groups = lax.axis_size("seq")
    parts = lax.axis_size("head")
    count = SEGS * groups
    scale = (channels // heads) ** (-0.5)
    rim = conv_taps.shape[0] // 2
    model_width = out_weight.shape[1]
    own_width = model_width // parts
    column_rows = model_width // groups
    rows_shape = (documents, tokens, channels)
    marks_shape = (documents, count, channels)
    pair_shape = (documents, tokens, 2 * count)
    units = 2 * documents
    saved = (ITERS, units, count, count)

    (sent,) = call(
        means_kernel, [((groups, 8, channels), f32)], queries, key_vectors, grant=60
    )
    own_grad, sent = lax.optimization_barrier((out_grad, sent))
    got = exchange(sent, "seq").reshape(groups * 8, channels)
    own_grad = own_grad.reshape(documents * tokens, own_width)
    rows = documents * tokens
    up, down, up_two, down_two, kept = call(
        functools.partial(pack_kernel, parts),
        [((rows + pieces * channels, own_width), bf16) for pieces in (1, 1, 3, 2)]
        + [((channels, own_width), bf16)],
        own_grad, out_weight,
        grant=60,
    )
    up_two, down_two = shift_by(up_two, 2, parts), shift_by(down_two, parts - 2, parts)
    up, down = shift_by(up, 1, parts), shift_by(down, parts - 1, parts)
    up_three = shift_by(up_two[channels : rows + 2 * channels], 1, parts)
    down_three = shift_by(down_two[: rows + channels], parts - 1, parts)
    across = shift_by(up_two[: rows + channels], 2, parts)
    og_parts = [own_grad, up, up_two, up_three, across, down_three, down_two, down]
    og_starts = (0, 0, channels, 0, channels, 0, 0, 0)
    w_starts = (0, rows, rows + 2 * channels, rows, 0, rows, rows + channels, rows)

    weights, scores, local_mixed, local_log, qm, km = call(
        functools.partial(stats_kernel, scale),
        [
            (pair_shape, f32),
            (pair_shape, f32),
            (marks_shape, f32),
            ((8, count), f32),
            (marks_shape, f32),
            (marks_shape, f32),
        ],
        got, queries, key_vectors, value_vectors,
    )
    sent, context_grad, first_rows, last_rows = call(
        functools.partial(chunk_kernel, parts, rim, og_starts),
        [((groups * 12, channels), f32), (rows_shape, f32)]
        + [((documents, 3 * rim, channels), bf16)] * 2,
        *og_parts, out_weight, value_vectors, weights, local_mixed, local_log,
    )
    sent, qm, km = lax.optimization_barrier((sent, qm, km))
    got = exchange(sent.reshape(groups, 3, 4, channels), "seq").reshape(groups * 12, channels)
    ends = groups - 1
    above = lax.ppermute(last_rows, "seq", [(i, i + 1) for i in range(ends)])
    below = lax.ppermute(first_rows, "seq", [(i + 1, i) for i in range(ends)])
    (inverse,) = call(
        functools.partial(inverse_kernel, scale), [((units, count, count), f32)], qm, km, flops=2e9
    )
    got, above, below, inverse = lax.optimization_barrier((got, above, below, inverse))
    sent, logs = call(
        combine_kernel, [((groups, 8, channels), f32), ((8, count), f32)], got
    )
    sent, og_parts = lax.optimization_barrier((sent, og_parts))
    (og_turned,) = call(
        functools.partial(turn_kernel, parts, og_starts), [((model_width, documents * tokens), bf16)], *og_parts
    )
    got = exchange(sent, "seq").reshape(groups * 8, channels)
    conv, back = call(
        conv_kernel,
        [(rows_shape, f32), (rows_shape, f32)],
        conv_taps, value_vectors, context_grad, above, below,
        scratch=[pltpu.VMEM((documents, tokens + 2 * rim, channels), f32)] * 2,
        smem=(0,),
        flops=1e9,
    )
    got, conv, back, og_turned = lax.optimization_barrier((got, conv, back, og_turned))
    weight_parts = [kept] + og_parts[1:]
    context_b, mixed, mix, landmark_mix = call(
        context_kernel,
        [
            ((documents * tokens, channels), bf16),
            (marks_shape, f32),
            (marks_shape, f32),
            ((documents, 2 * count, channels), f32),
        ],
        got, weights, inverse, conv,
        scratch=[
            pltpu.VMEM((units, count, count), f32),
            pltpu.VMEM(rows_shape, f32),
            pltpu.SemaphoreType.DMA((2,)),
        ],
        far=(2, 3),
        grant=60,
    )
    near = [shift_by(context_b, 1, parts), shift_by(context_b, parts - 1, parts)]
    sent_shape = (groups, 16 + column_rows, channels)
    (sent,) = call(
        functools.partial(main_kernel, scale),
        [(sent_shape, bf16)],
        logs, weights, scores, context_grad, inverse, queries, key_vectors, value_vectors,
        og_turned, context_b, mixed, mix, landmark_mix,
        scratch=[
            pltpu.VMEM(sent_shape, bf16),
            pltpu.VMEM((groups * 16, channels), f32),
            pltpu.SemaphoreType.DMA((2,)),
        ],
        far_out=True,
        grant=60,
        flops=1e9,
    )
    sent, near, mix = lax.optimization_barrier((sent, near, mix))
    got = exchange(sent, "seq")
    query_direct, key_direct, value_grad = call(
        functools.partial(direct_kernel, scale),
        [(rows_shape, f32), (rows_shape, f32), (rows_shape, bf16)],
        logs, weights, scores, context_grad, qm, km, inverse, value_vectors, back, mixed, mix,
        flops=1e9,
    )
    far = [
        shift_by(jnp.concatenate([near[0], context_b, near[1]], axis=0), 3, parts),
        shift_by(jnp.concatenate([near[0], context_b], axis=0), parts - 3, parts),
    ]
    (own,) = call(
        functools.partial(newton_back_kernel, scale),
        [((8, channels), f32)],
        qm, km, mixed, mix,
        scratch=[pltpu.VMEM((2 * documents, count, channels), f32)] + [pltpu.VMEM(saved, f32)] * 5,
        flops=5e9,
    )
    blocks = ((0, 0), (1, 0), (3, 2), (3, 1), (3, 0), (4, 1), (4, 0), (2, 0))
    slots = tuple((5 + shift, start) for shift, start in enumerate(w_starts))
    (layer_output,) = call(
        functools.partial(output_kernel, blocks, slots),
        [((documents * tokens, own_width), bf16)],
        context_b, *near, *far, *weight_parts,
    )
    query_grad, key_grad, weight_grad = call(
        finish_kernel,
        [(rows_shape, bf16), (rows_shape, bf16), ((column_rows, channels), f32)],
        got, own, query_direct, key_direct,
    )
    return (
        layer_output.reshape(documents, tokens, own_width),
        query_grad,
        key_grad,
        value_grad,
        weight_grad.T,
    )


def solution(mesh):
    in_specs = (
        P(None, "seq", "head"),
        P(None, "seq", "head"),
        P(None, "seq", "head"),
        P(None, "head"),
        P("head", None),
        P(None, "seq", "head"),
    )
    out_specs = (
        P(None, "seq", "head"),
        P(None, "seq", "head"),
        P(None, "seq", "head"),
        P(None, "seq", "head"),
        P("head", "seq"),
    )
    return jax.shard_map(shards, mesh=mesh, in_specs=in_specs, out_specs=out_specs, check_vma=False)
```

```python
import functools

import jax
import jax.numpy as jnp
from jax import lax
from jax.experimental import pallas as pl
from jax.experimental.pallas import tpu as pltpu
from jax.sharding import PartitionSpec as P

ITERS = 2
SEGS = 2
f32 = jnp.float32
bf16 = jnp.bfloat16
NN = (((1,), (0,)), ((), ()))
NT = (((1,), (1,)), ((), ()))


def dot(left, right, dims=NN):
    return lax.dot_general(left, right, dims, preferred_element_type=f32)


def halves(value):
    if value.dtype == bf16:
        return (value,)
    high = value.astype(bf16)
    return high, (value - high.astype(f32)).astype(bf16)


def prod(left, right, dims=NN):
    left = left if isinstance(left, tuple) else halves(left)
    right = right if isinstance(right, tuple) else halves(right)
    total = dot(left[0], right[0], dims)
    if len(right) > 1:
        total = total + dot(left[0], right[1], dims)
    if len(left) > 1:
        total = total + dot(left[1], right[0], dims)
    return total


def block_at(shift, parts):
    core = lax.rem(lax.axis_index("seq"), 2)
    step = jnp.where(core == 0, parts - shift, parts + shift)
    return lax.rem(lax.axis_index("head") + step, parts)


def first_head(shape):
    return lax.broadcasted_iota(jnp.int32, shape, 1) < shape[1] // 2


def stack(rows):
    mask = first_head(rows.shape)
    zero = jnp.zeros_like(rows)
    return jnp.concatenate([jnp.where(mask, rows, zero), jnp.where(mask, zero, rows)], axis=0)


def own_blocks(full):
    count = full.shape[0] // 2
    mask = first_head((count, full.shape[1]))
    zero = jnp.zeros((count, full.shape[1]), full.dtype)
    return jnp.concatenate(
        [jnp.where(mask, full[:count], zero), jnp.where(mask, zero, full[count:])], axis=0
    )


def pick(full):
    count = full.shape[0] // 2
    return jnp.where(first_head((count, full.shape[1])), full[:count], full[count:])


def marks(ref, row, groups, stride):
    return jnp.concatenate(
        [ref[pl.ds(row + seg, groups, stride=stride), :] for seg in range(SEGS)], axis=0
    )


def means_kernel(q_ref, k_ref, out_ref):
    documents, tokens, _ = q_ref.shape
    segment = tokens // SEGS
    rows = []
    for ref in (q_ref, k_ref):
        for doc in range(documents):
            for seg in range(SEGS):
                part = ref[doc, seg * segment : (seg + 1) * segment, :].astype(f32)
                rows.append(jnp.sum(part, axis=0, keepdims=True) * (1.0 / segment))
    block = jnp.concatenate(rows, axis=0)
    out_ref[...] = jnp.broadcast_to(block[None], out_ref.shape)


def stats_kernel(scale, got_ref, q_ref, k_ref, v_ref, t_ref, s_ref, o_ref, log_ref, qm_ref, km_ref):
    documents = q_ref.shape[0]
    groups = got_ref.shape[0] // 8
    count = SEGS * groups
    logs = []
    for doc in range(documents):
        qm = marks(got_ref, doc * SEGS, groups, 8)
        km = marks(got_ref, 4 + doc * SEGS, groups, 8)
        qm_ref[doc] = qm
        km_ref[doc] = km
        scores = prod(q_ref[doc], stack(km), NT) * scale
        for head in range(2):
            part = scores[:, head * count : (head + 1) * count]
            part = jnp.exp(part - jnp.max(part, axis=1, keepdims=True))
            t_ref[doc, :, head * count : (head + 1) * count] = part / jnp.sum(
                part, axis=1, keepdims=True
            )
        scores = prod(k_ref[doc], stack(qm), NT) * scale
        s_ref[doc] = scores
        peak = jnp.max(scores, axis=0, keepdims=True)
        part = jnp.exp(scores - peak)
        total = jnp.sum(part, axis=0, keepdims=True)
        o_ref[doc] = pick(prod((part / total).T, v_ref[doc]))
        log = peak + jnp.log(total)
        logs += [log[:, :count], log[:, count:]]
    logs.append(jnp.zeros((8 - len(logs), count), f32))
    log_ref[...] = jnp.concatenate(logs, axis=0)


def pack_kernel(parts, og_ref, w_ref, up_ref, down_ref, up_two_ref, down_two_ref, kept_ref):
    width = og_ref.shape[1]
    for ref, items in (
        (up_ref, (None, 1)),
        (down_ref, (None, 7)),
        (up_two_ref, (4, None, 3, 2)),
        (down_two_ref, (None, 5, 6)),
        (kept_ref, (0,)),
    ):
        row = 0
        for shift in items:
            if shift is None:
                block = og_ref[...]
            else:
                start = pl.multiple_of(block_at(-shift, parts) * width, width)
                block = w_ref[:, pl.ds(start, width)]
            ref[row : row + block.shape[0], :] = block
            row += block.shape[0]


def chunk_kernel(parts, rim, starts, *refs):
    og_refs = refs[:parts]
    w_ref, v_ref, t_ref, o_ref, log_ref = refs[parts : parts + 5]
    out_ref, cg_ref, head_ref, tail_ref = refs[parts + 5 :]
    documents, tokens, channels = cg_ref.shape
    groups = out_ref.shape[0] // 12
    width = w_ref.shape[1] // parts

    def columns(shift):
        return pl.ds(pl.multiple_of(block_at(shift, parts) * width, width), width)

    total = None
    for shift in range(parts):
        block = og_refs[shift][starts[shift] : starts[shift] + documents * tokens, :]
        part = dot(block, w_ref[:, columns(shift)], NT)
        total = part if total is None else total + part
    for doc in range(documents):
        grad = total[doc * tokens : (doc + 1) * tokens]
        cg_ref[doc] = grad
        for ref, rows in ((head_ref, slice(0, rim)), (tail_ref, slice(tokens - rim, tokens))):
            high, low = halves(grad[rows])
            ref[doc, 0:rim, :] = v_ref[doc, rows, :]
            ref[doc, rim : 2 * rim, :] = high
            ref[doc, 2 * rim : 3 * rim, :] = low
        mix = pick(prod(t_ref[doc].T, grad))
        for seg in range(SEGS):
            row = doc * SEGS + seg
            rows = slice(seg * groups, (seg + 1) * groups)
            out_ref[pl.ds(row, groups, stride=12), :] = o_ref[doc, rows, :]
            out_ref[pl.ds(4 + row, groups, stride=12), :] = mix[rows]
    for row in range(4):
        out_ref[pl.ds(8 + row, groups, stride=12), :] = jnp.broadcast_to(
            log_ref[row : row + 1, :], (groups, channels)
        )


def landmark_units(scale, qm_ref, km_ref):
    count = qm_ref.shape[1]
    units = []
    for doc in range(qm_ref.shape[0]):
        scores = prod(stack(qm_ref[doc]), km_ref[doc], NT) * scale
        scores = jnp.exp(scores - jnp.max(scores, axis=1, keepdims=True))
        scores = scores / jnp.sum(scores, axis=1, keepdims=True)
        units += [scores[:count], scores[count:]]
    return units


def column_peak(unit):
    return jnp.max(jnp.sum(unit, axis=0, keepdims=True), axis=1, keepdims=True)


def newton(units, keep):
    every = range(len(units))
    count = units[0].shape[0]
    row = lax.broadcasted_iota(jnp.int32, (count, count), 0)
    identity = (row == lax.broadcasted_iota(jnp.int32, (count, count), 1)).astype(f32)
    approx = [unit.T / column_peak(unit) for unit in units]
    units = [halves(unit) for unit in units]
    for step in range(ITERS):
        spread = [halves(approx[i]) for i in every]
        product = [prod(units[i], spread[i]) for i in every]
        first = [7.0 * identity - product[i] for i in every]
        split = [halves(product[i]) for i in every]
        second = [15.0 * identity - prod(split[i], first[i]) for i in every]
        third = [13.0 * identity - prod(split[i], second[i]) for i in every]
        for i in every:
            keep(step, i, (approx[i], product[i], first[i], second[i], third[i]))
        if step < ITERS - 1 or not keep.last:
            approx = [0.25 * prod(spread[i], third[i]) for i in every]
    return approx


class Nothing:
    last = False

    def __call__(self, step, index, values):
        pass


class Kept:
    last = True

    def __init__(self, refs):
        self.refs = refs

    def __call__(self, step, index, values):
        for ref, value in zip(self.refs, values):
            ref[step, index] = value.T


def inverse_kernel(scale, qm_ref, km_ref, inv_ref):
    for index, unit in enumerate(newton(landmark_units(scale, qm_ref, km_ref), Nothing())):
        inv_ref[index] = unit


def turn_kernel(parts, starts, *refs):
    count, width = refs[parts].shape[1], refs[0].shape[1]
    for shift in range(parts):
        start = pl.multiple_of(block_at(shift, parts) * width, width)
        refs[parts][pl.ds(start, width), :] = refs[shift][starts[shift] : starts[shift] + count, :].T


def combine_kernel(got_ref, out_ref, log_ref):
    groups = got_ref.shape[0] // 12
    channels = got_ref.shape[1]
    me = lax.axis_index("seq")
    lane = lax.broadcasted_iota(jnp.int32, (groups, channels), 1)
    shares, logs = [], []
    for unit in range(4):
        log = got_ref[pl.ds(8 + unit, groups, stride=12), :]
        top = jnp.max(log, axis=0, keepdims=True)
        part = jnp.exp(log - top)
        total = jnp.sum(part, axis=0, keepdims=True)
        logs.append(top + jnp.log(total))
        shares.append(part / total)
    logs.append(jnp.zeros((4, channels), f32))
    log_ref[...] = jnp.concatenate(logs, axis=0)
    mixed, mix = [], []
    for doc in range(2):
        for seg in range(SEGS):
            row = doc * SEGS + seg
            weight = [
                jnp.sum(
                    jnp.where(lane == seg * groups + me, shares[doc * 2 + head], 0.0),
                    axis=1,
                    keepdims=True,
                )
                for head in range(2)
            ]
            weight = jnp.where(lane < channels // 2, weight[0], weight[1])
            mixed.append(
                jnp.sum(weight * got_ref[pl.ds(row, groups, stride=12), :], axis=0, keepdims=True)
            )
            mix.append(jnp.sum(got_ref[pl.ds(4 + row, groups, stride=12), :], axis=0, keepdims=True))
    block = jnp.concatenate(mixed + mix, axis=0)
    out_ref[...] = jnp.broadcast_to(block[None], out_ref.shape)


def conv_kernel(taps_ref, v_ref, cg_ref, above_ref, below_ref, conv_ref, back_ref, vp, cp):
    documents, tokens, channels = v_ref.shape
    taps = taps_ref.shape[0]
    rim = taps // 2
    for doc in range(documents):
        vp[doc, rim : rim + tokens, :] = v_ref[doc].astype(f32)
        cp[doc, rim : rim + tokens, :] = cg_ref[doc]
        for ref, start in ((above_ref, 0), (below_ref, rim + tokens)):
            rows = [ref[doc, i * rim : (i + 1) * rim, :].astype(f32) for i in range(3)]
            vp[doc, start : start + rim, :] = rows[0]
            cp[doc, start : start + rim, :] = rows[1] + rows[2]
    lane = lax.broadcasted_iota(jnp.int32, (1, channels), 1)
    for doc in range(documents):
        conv = jnp.zeros((tokens, channels), f32)
        back = jnp.zeros((tokens, channels), f32)
        for tap in range(taps):
            weight = jnp.where(lane < channels // 2, taps_ref[tap, 0], taps_ref[tap, 1])
            conv = conv + weight * vp[doc, tap : tap + tokens, :]
            start = 2 * rim - tap
            back = back + weight * cp[doc, start : start + tokens, :]
        conv_ref[doc] = conv
        back_ref[doc] = back


def context_kernel(
    got_ref, t_ref, inv_far, conv_far, ctx_ref, mixed_ref, mix_ref, lm_ref, inv_ref, conv_ref, sems
):
    fetches = [
        pltpu.make_async_copy(inv_far, inv_ref, sems.at[0]),
        pltpu.make_async_copy(conv_far, conv_ref, sems.at[1]),
    ]
    for fetch in fetches:
        fetch.start()
    for fetch in fetches:
        fetch.wait()
    documents, tokens, _ = conv_ref.shape
    groups = got_ref.shape[0] // 8
    for doc in range(documents):
        mixed = marks(got_ref, doc * SEGS, groups, 8)
        mixed_ref[doc] = mixed
        mix_ref[doc] = marks(got_ref, 4 + doc * SEGS, groups, 8)
        inverse = jnp.concatenate([inv_ref[doc * 2], inv_ref[doc * 2 + 1]], axis=0)
        landmark = own_blocks(prod(inverse, mixed))
        lm_ref[doc] = landmark
        ctx = (prod(t_ref[doc], landmark) + conv_ref[doc]).astype(bf16)
        ctx_ref[doc * tokens : (doc + 1) * tokens, :] = ctx


def token_back(scale, weights, grad, landmark):
    count = weights.shape[1] // 2
    back = weights * prod(grad, landmark, NT)
    return jnp.concatenate(
        [
            back[:, part] - weights[:, part] * jnp.sum(back[:, part], axis=1, keepdims=True)
            for part in (slice(0, count), slice(count, 2 * count))
        ],
        axis=1,
    ) * scale


def key_side(scale, doc, log_ref, s_ref, inv_ref, v_ref, mixed_ref, mix_ref):
    turned = jnp.concatenate([inv_ref[doc * 2].T, inv_ref[doc * 2 + 1].T], axis=0)
    mixed_grad = own_blocks(prod(turned, mix_ref[doc]))
    ones = jnp.ones((8, mixed_grad.shape[1]), bf16)
    mixed_dot = prod(ones, mixed_grad * stack(mixed_ref[doc]), NT)[0:1]
    mixed_grad = halves(mixed_grad)
    log = jnp.concatenate(
        [log_ref[doc * 2 : doc * 2 + 1, :], log_ref[doc * 2 + 1 : doc * 2 + 2, :]], axis=1
    )
    key_weights = jnp.exp(s_ref[doc] - log)
    key_back = key_weights * (prod(v_ref[doc], mixed_grad, NT) - mixed_dot) * scale
    return key_weights, key_back, mixed_grad


def main_kernel(
    scale, log_ref, t_ref, s_ref, cg_ref, inv_ref, q_ref, k_ref, v_ref, ogt_ref, ctx_ref,
    mixed_ref, mix_ref, lm_ref, out_far, out_ref, held, sems,
):
    documents, tokens, channels = q_ref.shape
    groups = out_ref.shape[0]
    terms = dot(ogt_ref[...], ctx_ref[...]).astype(bf16)
    out_ref[:, 16:, :] = terms.reshape(groups, terms.shape[0] // groups, channels)
    rest = pltpu.make_async_copy(out_ref.at[:, 16:, :], out_far.at[:, 16:, :], sems.at[0])
    rest.start()
    for doc in range(documents):
        back = token_back(scale, t_ref[doc], cg_ref[doc], lm_ref[doc])
        key_terms = pick(prod(back.T, q_ref[doc]))
        _, key_back, _ = key_side(scale, doc, log_ref, s_ref, inv_ref, v_ref, mixed_ref, mix_ref)
        query_terms = pick(prod(key_back.T, k_ref[doc]))
        for base, terms in ((0, query_terms), (4, key_terms)):
            high = terms.astype(bf16).astype(f32)
            low = terms - high
            for seg in range(SEGS):
                row = base + doc * SEGS + seg
                rows = slice(seg * groups, (seg + 1) * groups)
                held[pl.ds(row, groups, stride=16), :] = high[rows]
                held[pl.ds(8 + row, groups, stride=16), :] = low[rows]
    out_ref[:, 0:16, :] = held[...].astype(bf16).reshape(groups, 16, channels)
    first = pltpu.make_async_copy(out_ref.at[:, 0:16, :], out_far.at[:, 0:16, :], sems.at[1])
    first.start()
    rest.wait()
    first.wait()


def direct_kernel(
    scale, log_ref, t_ref, s_ref, cg_ref, qm_ref, km_ref, inv_ref, v_ref, back_ref, mixed_ref,
    mix_ref, qd_ref, kd_ref, vg_ref,
):
    for doc in range(v_ref.shape[0]):
        inverse = jnp.concatenate([inv_ref[doc * 2], inv_ref[doc * 2 + 1]], axis=0)
        landmark = own_blocks(prod(inverse, mixed_ref[doc]))
        back = token_back(scale, t_ref[doc], cg_ref[doc], landmark)
        qd_ref[doc] = prod(back, stack(km_ref[doc]))
        key_weights, key_back, mixed_grad = key_side(
            scale, doc, log_ref, s_ref, inv_ref, v_ref, mixed_ref, mix_ref
        )
        kd_ref[doc] = prod(key_back, stack(qm_ref[doc]))
        vg_ref[doc] = (prod(key_weights, mixed_grad) + back_ref[doc]).astype(bf16)


def newton_back_kernel(scale, qm_ref, km_ref, mixed_ref, mix_ref, out_ref, held, *kept):
    documents, count, channels = qm_ref.shape
    me = lax.axis_index("seq")
    groups = count // SEGS
    every = range(documents * 2)
    units = landmark_units(scale, qm_ref, km_ref)
    newton(units, Kept(kept))
    approx_t, product_t, first_t, second_t, third_t = kept
    down = []
    for doc in range(documents):
        full = prod(stack(mix_ref[doc]), mixed_ref[doc], NT)
        down += [full[:count], full[count:]]
    unit_t = [halves(units[i].T) for i in every]
    grads = [None for i in every]
    for step in reversed(range(ITERS)):
        down = [halves(0.25 * down[i]) for i in every]
        turned = [halves(approx_t[step, i]) for i in every]
        product = [halves(product_t[step, i]) for i in every]
        third = [prod(turned[i], down[i]) for i in every]
        third = [halves(third[i]) for i in every]
        carry = [prod(down[i], third_t[step, i]) for i in every]
        second = [-prod(product[i], third[i]) for i in every]
        second = [halves(second[i]) for i in every]
        first = [-prod(product[i], second[i]) for i in every]
        flow = [
            -first[i] - prod(third[i], second_t[step, i]) - prod(second[i], first_t[step, i])
            for i in every
        ]
        flow = [halves(flow[i]) for i in every]
        more = [prod(flow[i], turned[i]) for i in every]
        grads = [more[i] if grads[i] is None else grads[i] + more[i] for i in every]
        down = [carry[i] + prod(unit_t[i], flow[i]) for i in every]
    for doc in range(documents):
        back, turned = [], []
        for head in range(2):
            i = doc * 2 + head
            unit = units[i]
            grad = grads[i] + down[i].T / column_peak(unit)
            part = unit * grad
            part = (part - unit * jnp.sum(part, axis=1, keepdims=True)) * scale
            back.append(part)
            turned.append(part.T)
        held[doc] = pick(prod(jnp.concatenate(back, axis=0), km_ref[doc]))
        held[documents + doc] = pick(prod(jnp.concatenate(turned, axis=0), qm_ref[doc]))
    for kind in range(2 * documents):
        for seg in range(SEGS):
            out_row = kind * SEGS + seg
            out_ref[out_row : out_row + 1, :] = held[kind, pl.ds(seg * groups + me, 1), :]


def finish_kernel(got_ref, own_ref, qd_ref, kd_ref, qg_ref, kg_ref, wg_ref):
    documents, tokens, _ = qd_ref.shape
    segment = tokens // SEGS
    total = jnp.sum(got_ref[:, 0:16, :].astype(f32), axis=0)
    total = (total[0:8] + total[8:16] + own_ref[...]) * (1.0 / segment)
    for base, source, target in ((0, qd_ref, qg_ref), (4, kd_ref, kg_ref)):
        for doc in range(documents):
            for seg in range(SEGS):
                row = base + doc * SEGS + seg
                rows = slice(seg * segment, (seg + 1) * segment)
                target[doc, rows, :] = (source[doc, rows, :] + total[row : row + 1]).astype(bf16)
    wg_ref[...] = jnp.sum(got_ref[:, 16:, :].astype(f32), axis=0)


def output_kernel(blocks, weights, *refs):
    total = None
    tokens = refs[-1].shape[0]
    channels = refs[0].shape[1]
    for (index, block), (source, row) in zip(blocks, weights):
        weight = refs[source][row : row + channels, :]
        part = dot(refs[index][block * tokens : (block + 1) * tokens, :], weight)
        total = part if total is None else total + part
    refs[-1][...] = total.astype(bf16)


def call(kernel, outs, *operands, scratch=(), smem=(), far=(), far_out=False, grant=16, flops=1e8, size=2e6):
    vmem = pl.BlockSpec(memory_space=pltpu.VMEM)
    scalar = pl.BlockSpec(memory_space=pltpu.SMEM)
    anywhere = pl.BlockSpec(memory_space=pl.ANY)
    return pl.pallas_call(
        kernel,
        out_shape=[jax.ShapeDtypeStruct(shape, kind) for shape, kind in outs],
        in_specs=[
            scalar if i in smem else anywhere if i in far else vmem for i in range(len(operands))
        ],
        out_specs=[anywhere if far_out else vmem for _ in outs],
        scratch_shapes=list(scratch),
        compiler_params=pltpu.CompilerParams(vmem_limit_bytes=grant * 1024 * 1024),
        cost_estimate=pl.CostEstimate(
            flops=int(flops), bytes_accessed=int(size), transcendentals=0
        ),
    )(*operands)


def exchange(blocks, axis):
    return lax.all_to_all(blocks, axis, 0, 0, tiled=True)


def shift_by(block, shift, parts):
    pairs = []
    for i in range(lax.axis_size("seq")):
        step = shift if i % 2 == 0 else parts - shift
        pairs += [(i * parts + j, i * parts + (j + step) % parts) for j in range(parts)]
    return lax.ppermute(block, ("seq", "head"), pairs)


def shards(queries, key_vectors, value_vectors, conv_taps, out_weight, out_grad):
    documents, tokens, channels = queries.shape
    heads = conv_taps.shape[1]
    groups = lax.axis_size("seq")
    parts = lax.axis_size("head")
    count = SEGS * groups
    scale = (channels // heads) ** (-0.5)
    rim = conv_taps.shape[0] // 2
    model_width = out_weight.shape[1]
    own_width = model_width // parts
    column_rows = model_width // groups
    rows_shape = (documents, tokens, channels)
    marks_shape = (documents, count, channels)
    pair_shape = (documents, tokens, 2 * count)
    units = 2 * documents
    saved = (ITERS, units, count, count)

    (sent,) = call(
        means_kernel, [((groups, 8, channels), f32)], queries, key_vectors, grant=60
    )
    own_grad, sent = lax.optimization_barrier((out_grad, sent))
    got = exchange(sent, "seq").reshape(groups * 8, channels)
    own_grad = own_grad.reshape(documents * tokens, own_width)
    rows = documents * tokens
    up, down, up_two, down_two, kept = call(
        functools.partial(pack_kernel, parts),
        [((rows + pieces * channels, own_width), bf16) for pieces in (1, 1, 3, 2)]
        + [((channels, own_width), bf16)],
        own_grad, out_weight,
        grant=60,
    )
    up_two, down_two = shift_by(up_two, 2, parts), shift_by(down_two, parts - 2, parts)
    up, down = shift_by(up, 1, parts), shift_by(down, parts - 1, parts)
    up_three = shift_by(up_two[channels : rows + 2 * channels], 1, parts)
    down_three = shift_by(down_two[: rows + channels], parts - 1, parts)
    across = shift_by(up_two[: rows + channels], 2, parts)
    og_parts = [own_grad, up, up_two, up_three, across, down_three, down_two, down]
    og_starts = (0, 0, channels, 0, channels, 0, 0, 0)
    w_starts = (0, rows, rows + 2 * channels, rows, 0, rows, rows + channels, rows)

    weights, scores, local_mixed, local_log, qm, km = call(
        functools.partial(stats_kernel, scale),
        [
            (pair_shape, f32),
            (pair_shape, f32),
            (marks_shape, f32),
            ((8, count), f32),
            (marks_shape, f32),
            (marks_shape, f32),
        ],
        got, queries, key_vectors, value_vectors,
    )
    sent, context_grad, first_rows, last_rows = call(
        functools.partial(chunk_kernel, parts, rim, og_starts),
        [((groups * 12, channels), f32), (rows_shape, f32)]
        + [((documents, 3 * rim, channels), bf16)] * 2,
        *og_parts, out_weight, value_vectors, weights, local_mixed, local_log,
    )
    sent, qm, km = lax.optimization_barrier((sent, qm, km))
    got = exchange(sent.reshape(groups, 3, 4, channels), "seq").reshape(groups * 12, channels)
    ends = groups - 1
    above = lax.ppermute(last_rows, "seq", [(i, i + 1) for i in range(ends)])
    below = lax.ppermute(first_rows, "seq", [(i + 1, i) for i in range(ends)])
    (inverse,) = call(
        functools.partial(inverse_kernel, scale), [((units, count, count), f32)], qm, km, flops=2e9
    )
    got, above, below, inverse = lax.optimization_barrier((got, above, below, inverse))
    sent, logs = call(
        combine_kernel, [((groups, 8, channels), f32), ((8, count), f32)], got
    )
    sent, og_parts = lax.optimization_barrier((sent, og_parts))
    (og_turned,) = call(
        functools.partial(turn_kernel, parts, og_starts), [((model_width, documents * tokens), bf16)], *og_parts
    )
    got = exchange(sent, "seq").reshape(groups * 8, channels)
    conv, back = call(
        conv_kernel,
        [(rows_shape, f32), (rows_shape, f32)],
        conv_taps, value_vectors, context_grad, above, below,
        scratch=[pltpu.VMEM((documents, tokens + 2 * rim, channels), f32)] * 2,
        smem=(0,),
        flops=1e9,
    )
    got, conv, back, og_turned = lax.optimization_barrier((got, conv, back, og_turned))
    weight_parts = [kept] + og_parts[1:]
    context_b, mixed, mix, landmark_mix = call(
        context_kernel,
        [
            ((documents * tokens, channels), bf16),
            (marks_shape, f32),
            (marks_shape, f32),
            ((documents, 2 * count, channels), f32),
        ],
        got, weights, inverse, conv,
        scratch=[
            pltpu.VMEM((units, count, count), f32),
            pltpu.VMEM(rows_shape, f32),
            pltpu.SemaphoreType.DMA((2,)),
        ],
        far=(2, 3),
    )
    near = [shift_by(context_b, 1, parts), shift_by(context_b, parts - 1, parts)]
    sent_shape = (groups, 16 + column_rows, channels)
    (sent,) = call(
        functools.partial(main_kernel, scale),
        [(sent_shape, bf16)],
        logs, weights, scores, context_grad, inverse, queries, key_vectors, value_vectors,
        og_turned, context_b, mixed, mix, landmark_mix,
        scratch=[
            pltpu.VMEM(sent_shape, bf16),
            pltpu.VMEM((groups * 16, channels), f32),
            pltpu.SemaphoreType.DMA((2,)),
        ],
        far_out=True,
        flops=1e9,
    )
    sent, near, mix = lax.optimization_barrier((sent, near, mix))
    got = exchange(sent, "seq")
    query_direct, key_direct, value_grad = call(
        functools.partial(direct_kernel, scale),
        [(rows_shape, f32), (rows_shape, f32), (rows_shape, bf16)],
        logs, weights, scores, context_grad, qm, km, inverse, value_vectors, back, mixed, mix,
        flops=1e9,
    )
    far = [
        shift_by(jnp.concatenate([near[0], context_b, near[1]], axis=0), 3, parts),
        shift_by(jnp.concatenate([near[0], context_b], axis=0), parts - 3, parts),
    ]
    (own,) = call(
        functools.partial(newton_back_kernel, scale),
        [((8, channels), f32)],
        qm, km, mixed, mix,
        scratch=[pltpu.VMEM((2 * documents, count, channels), f32)] + [pltpu.VMEM(saved, f32)] * 5,
        flops=5e9,
    )
    blocks = ((0, 0), (1, 0), (3, 2), (3, 1), (3, 0), (4, 1), (4, 0), (2, 0))
    slots = tuple((5 + shift, start) for shift, start in enumerate(w_starts))
    (layer_output,) = call(
        functools.partial(output_kernel, blocks, slots),
        [((documents * tokens, own_width), bf16)],
        context_b, *near, *far, *weight_parts,
    )
    query_grad, key_grad, weight_grad = call(
        finish_kernel,
        [(rows_shape, bf16), (rows_shape, bf16), ((column_rows, channels), f32)],
        got, own, query_direct, key_direct,
    )
    return (
        layer_output.reshape(documents, tokens, own_width),
        query_grad,
        key_grad,
        value_grad,
        weight_grad.T,
    )


def solution(mesh):
    in_specs = (
        P(None, "seq", "head"),
        P(None, "seq", "head"),
        P(None, "seq", "head"),
        P(None, "head"),
        P("head", None),
        P(None, "seq", "head"),
    )
    out_specs = (
        P(None, "seq", "head"),
        P(None, "seq", "head"),
        P(None, "seq", "head"),
        P(None, "seq", "head"),
        P("head", "seq"),
    )
    return jax.shard_map(shards, mesh=mesh, in_specs=in_specs, out_specs=out_specs, check_vma=False)
```
